512 devices in a mesh: freq: 128 (over y, x_lo, z), tile: 4 (over x_hi, core).
Axes of the slice: x: 4 (x_hi: 2, x_lo: 2; x = x_hi * 2 + x_lo), y: 8, z: 8, core: 2. Of those that a mesh axis runs over, the one named last changes fastest.
Arguments:
- wavefield: bfloat16 [2, 128, 512, 512], P(None, None, 'freq', 'tile'), may hold values from -6 to 6
- slowness: bfloat16 [128, 512, 512], P('freq', 'tile'), may hold values from 0.69921875 to 1.3984375
- freq_ids: int32 [128], replicated, may hold values from 0 to 127, each once
- depth_owner: int32 [1], replicated, may hold values from 0 to 127
Outputs:
- wave_next: bfloat16 [2, 128, 512, 512], P(None, 'freq', 'tile')
- image: float32 [512, 512], P('tile', 'freq')
The draws below stay inside these ranges and needn't reach their ends.
Inputs may be any that keep to these rules, and one draw needn't show every extreme that they name: `freq_ids`: each frequency number appears in exactly one slot.
All inputs are finite; a program needn't handle non-finite values.
Results may differ from the reference program's by a relative error of at most 0.0097.
Values may be sent and summed in bfloat16 or wider, within the bound.
No kernel may reach another device: no remote copies, remote signals or barrier semaphores. Data moves between devices by JAX's collectives and lax.ppermute only.
A program may use at most 64 MiB of HBM per device.

```python
import math
import jax
import jax.numpy as jnp
from jax import lax

NX = 512
NY = 512
NF = 128
DEPTHS = 128
N_FREQ = 128


def block_scale(own_key, dims, shards, least, largest):
    loudness = 1.0
    for axis_at, parts in shards:
        heights = jax.random.uniform(jax.random.fold_in(jax.random.fold_in(own_key, 6), axis_at), (parts,), jnp.float32, least / len(shards), largest / len(shards))
        loudness = loudness * jnp.repeat(jnp.exp(heights), dims[axis_at] // parts).reshape((-1,) + (1,) * (len(dims) - 1 - axis_at))
    return loudness


def gaussian(key, extent, scale, reach, pieces=(), held_as=jnp.bfloat16):
    result = scale * jax.random.normal(key, extent, jnp.float32)
    if pieces:
        result = result * block_scale(key, extent, pieces, -0.22, 0.18)
    return jnp.clip(result, -reach, reach).astype(held_as)


def setup_inputs(seed: int = 0) -> dict:
    splits = jax.random.split(jax.random.key(seed), 5)
    wavefield = gaussian(splits[0], (2, NF, NX, NY), 1.0, 6.0, ((2, 128), (3, 4)))
    slowness = jnp.clip(jnp.exp(math.log(1.3984375) - 0.6931472 * jax.random.uniform(splits[1], (DEPTHS, NX, NY), jnp.float32) ** block_scale(splits[1], (DEPTHS, NX, NY), ((0, 128), (1, 4)), -0.2, 0.2)), 0.69921875, 1.3984375).astype(jnp.bfloat16)
    freq_ids = jax.random.permutation(splits[2], NF).astype(jnp.int32)
    depth_owner = jax.random.randint(splits[3], (1,), 0, N_FREQ).astype(jnp.int32)
    return dict(wavefield=wavefield, slowness=slowness, freq_ids=freq_ids, depth_owner=depth_owner)


depth_step = 0.5
omega_top = 2.8

def dft_table(length):
    places = jnp.arange(length, dtype=jnp.int32)
    product = places[:, None] * places[None, :] % length
    angles = 2.0 * math.pi / length * product.astype(jnp.float32)
    factor = 1.0 / math.sqrt(length)
    return ((jnp.cos(angles) * factor).astype(jnp.bfloat16), (jnp.sin(angles) * factor).astype(jnp.bfloat16))

def wavenumbers(length):
    places = jnp.arange(length, dtype=jnp.int32)
    signed = jnp.where(places < length // 2, places, places - length)
    return 2.0 * math.pi / length * signed.astype(jnp.float32)

def matmul(left, right):
    return jnp.dot(left.astype(jnp.float32), right.astype(jnp.float32), precision=lax.Precision.HIGHEST)

def reference(wavefield, slowness, freq_ids, depth_owner):
    slowness_now = lax.dynamic_index_in_dim(slowness, depth_owner[0], 0, keepdims=False).astype(jnp.float32)
    xcos, xsin = dft_table(NX)
    ycos, ysin = dft_table(NY)
    kx_square = (wavenumbers(NX) ** 2)[:, None]
    ky_square = (wavenumbers(NY) ** 2)[None, :]
    count = freq_ids.shape[0]

    def one_slot(image_sum, inputs):
        slot_wave, slot_id = inputs
        angular = omega_top * (slot_id + 1).astype(jnp.float32) / count
        phase = angular * depth_step * (slowness_now - 1.0)
        lens_cos = jnp.cos(phase)
        lens_sin = jnp.sin(phase)
        wave_real = slot_wave[0].astype(jnp.float32)
        wave_imag = slot_wave[1].astype(jnp.float32)
        lensed_real = (wave_real * lens_cos - wave_imag * lens_sin).astype(jnp.bfloat16)
        lensed_imag = (wave_real * lens_sin + wave_imag * lens_cos).astype(jnp.bfloat16)
        half_real = (matmul(lensed_real, ycos) + matmul(lensed_imag, ysin)).astype(jnp.bfloat16)
        half_imag = (matmul(lensed_imag, ycos) - matmul(lensed_real, ysin)).astype(jnp.bfloat16)
        spec_real = matmul(xcos, half_real) + matmul(xsin, half_imag)
        spec_imag = matmul(xcos, half_imag) - matmul(xsin, half_real)
        vertical = angular * angular - kx_square - ky_square
        travel = depth_step * jnp.sqrt(jnp.maximum(vertical, 0.0))
        damping = jnp.exp(-depth_step * jnp.sqrt(jnp.maximum(-vertical, 0.0)))
        shift_real = damping * jnp.cos(travel)
        shift_imag = damping * jnp.sin(travel)
        shifted_real = (spec_real * shift_real - spec_imag * shift_imag).astype(jnp.bfloat16)
        shifted_imag = (spec_real * shift_imag + spec_imag * shift_real).astype(jnp.bfloat16)
        back_real = (matmul(xcos, shifted_real) - matmul(xsin, shifted_imag)).astype(jnp.bfloat16)
        back_imag = (matmul(xcos, shifted_imag) + matmul(xsin, shifted_real)).astype(jnp.bfloat16)
        field_real = matmul(back_real, ycos) - matmul(back_imag, ysin)
        field_imag = matmul(back_imag, ycos) + matmul(back_real, ysin)
        stacked = jnp.stack([field_real, field_imag]).astype(jnp.bfloat16)
        return (image_sum + field_real, stacked)
    start = jnp.zeros((NX, NY), jnp.float32)
    image_sum, fields = lax.scan(one_slot, start, (jnp.moveaxis(wavefield, 1, 0), freq_ids))
    wave_next = jnp.moveaxis(fields, 0, 1)
    image = image_sum / math.sqrt(count)
    return (wave_next, image)
```

```python
import math

import jax
import jax.numpy as jnp
import numpy as np
from jax import lax
from jax.experimental import pallas as pl
from jax.experimental.pallas import tpu as pltpu
from jax.sharding import Mesh
from jax.sharding import PartitionSpec as P

depth_step = 0.5
omega_top = 2.8
slots = 128
size = 512
tile_size = 128
freq = ("u", "v", "w", "z", "l")


def dft_table(length):
    places = np.arange(length)
    angles = 2.0 * np.pi / length * (places[:, None] * places[None, :] % length)
    factor = 1.0 / math.sqrt(length)
    return (
        (np.cos(angles) * factor).astype(jnp.bfloat16),
        (np.sin(angles) * factor).astype(jnp.bfloat16),
    )


def dot(left, right):
    return jnp.dot(left, right, preferred_element_type=jnp.float32)


def series(square, first, last):
    total = (-1.0) ** ((last - first) // 2) / math.factorial(last)
    for order in range(last - 2, first - 1, -2):
        total = (-1.0) ** ((order - first) // 2) / math.factorial(order) + square * total
    return total


def pick_kernel(owner_ref, rows_ref, out_ref):
    rows = rows_ref[owner_ref[0] // 2 % 16].astype(jnp.float32)
    for l in range(2):
        for c in range(2):
            lanes = (c * tile_size, (2 + c) * tile_size)
            piece = jnp.concatenate([rows[4 * l : 4 * l + 4, lane : lane + tile_size] for lane in lanes], axis=0)
            piece = piece.astype(jnp.bfloat16)
            for u in range(4):
                for h in range(2):
                    out_ref[((u * 2 + l) * 2 + h) * 2 + c] = piece


def shift_kernel(slot_ref, ids_ref, shift_ref):
    angular = omega_top * (ids_ref[slot_ref[0]] + 1).astype(jnp.float32) / slots

    def square(start, shape, axis):
        places = lax.broadcasted_iota(jnp.int32, shape, axis) + start
        signed = jnp.where(places < size // 2, places, places - size)
        return (2.0 * math.pi / size * signed.astype(jnp.float32)) ** 2

    ky_square = square(0, (16, size), 1)

    @pl.loop(0, size, step=16)
    def _(start):
        start = pl.multiple_of(start, 16)
        vertical = angular * angular - square(start, (16, size), 0) - ky_square
        root = depth_step * jnp.sqrt(jnp.abs(vertical))
        travel = jnp.where(vertical > 0.0, root, 0.0)
        damping = jnp.exp(jnp.where(vertical < 0.0, -root, 0.0))
        travel_square = travel * travel
        shift_ref[0, pl.ds(start, 16), :] = (damping * series(travel_square, 0, 12)).astype(jnp.bfloat16)
        shift_ref[1, pl.ds(start, 16), :] = (damping * travel * series(travel_square, 1, 13)).astype(jnp.bfloat16)


def pack_kernel(ids_ref, own_ref, other_ref, own_out, other_out, factor_ref):
    own_out[...] = own_ref[...]
    other_out[...] = other_ref[...]
    first = lax.broadcasted_iota(jnp.int32, (8, tile_size), 0) < 4
    for pair in range(slots // 2):
        low, high = (
            depth_step * (omega_top * (ids_ref[2 * pair + at] + 1).astype(jnp.float32) / slots) for at in range(2)
        )
        factor_ref[pair] = jnp.where(first, low, high)


def lens_kernel(place_ref, slow_ref, own_ref, other_ref, factor_ref, out_ref):
    slow = slow_ref[place_ref[0]].astype(jnp.float32) - 1.0
    halves = (jnp.concatenate([slow[:4]] * 2, axis=0), jnp.concatenate([slow[4:]] * 2, axis=0))
    low = place_ref[1] == 0
    depths = (jnp.where(low, halves[0], halves[1]), jnp.where(low, halves[1], halves[0]))
    for pair in range(slots // 2):
        factor = factor_ref[pair]
        for block, (ref, depth) in enumerate(zip((own_ref, other_ref), depths)):
            phase = factor * depth
            square = phase * phase
            lens_cos = series(square, 0, 8)
            lens_sin = phase * series(square, 1, 9)
            wave_real = ref[0, pair].astype(jnp.float32)
            wave_imag = ref[1, pair].astype(jnp.float32)
            real = wave_real * lens_cos - wave_imag * lens_sin
            imag = wave_real * lens_sin + wave_imag * lens_cos
            lanes = slice(block * tile_size, (block + 1) * tile_size)
            out_ref[2 * pair, :, lanes] = jnp.concatenate([real[:4], imag[:4]], axis=0).astype(jnp.bfloat16)
            out_ref[2 * pair + 1, :, lanes] = jnp.concatenate([real[4:], imag[4:]], axis=0).astype(jnp.bfloat16)


def column_kernel(cos_ref, sin_ref, wave_ref, out_ref, both):
    for at in range(0, size // 4, 4):
        tiles = [wave_ref[at + k].astype(jnp.float32) for k in range(4)]
        for part in range(2):
            rows = jnp.concatenate([tile[4 * part : 4 * part + 4] for tile in tiles], axis=0)
            both[4 * at : 4 * at + 16, part * 2 * tile_size : (part + 1) * 2 * tile_size] = rows.astype(jnp.bfloat16)
    by_cos = dot(cos_ref[...], both[...])
    by_sin = dot(sin_ref[...], both[...])
    real = (by_cos[:, : 2 * tile_size] + by_sin[:, 2 * tile_size :]).astype(jnp.bfloat16)
    imag = (by_cos[:, 2 * tile_size :] - by_sin[:, : 2 * tile_size]).astype(jnp.bfloat16)
    for block in range(2):
        lanes = slice(block * tile_size, (block + 1) * tile_size)
        out_ref[block, 0] = real[:, lanes]
        out_ref[block, 1] = imag[:, lanes]


def step_kernel(tile_ref, own_ref, other_ref, cos_ref, sin_ref, shift_ref, wave_ref, image_ref, field, back):
    tile = tile_ref[0]
    for flip in range(4):
        block = (own_ref, other_ref)[flip % 2]
        start = pl.multiple_of((tile ^ flip) * tile_size, tile_size)
        field[:, :, pl.ds(start, tile_size)] = block[flip // 2]
    rows = pl.ds(pl.multiple_of(tile * tile_size, tile_size), tile_size)
    inverse = jnp.concatenate([cos_ref[rows, :], sin_ref[rows, :]], axis=0)
    width = 256
    for at in range(0, size, width):
        part = slice(at, at + width)
        spec_real = dot(field[0], cos_ref[:, part]) + dot(field[1], sin_ref[:, part])
        spec_imag = dot(field[1], cos_ref[:, part]) - dot(field[0], sin_ref[:, part])
        shift_real = shift_ref[0, :, part].astype(jnp.float32)
        shift_imag = shift_ref[1, :, part].astype(jnp.float32)
        shifted_real = (spec_real * shift_real - spec_imag * shift_imag).astype(jnp.bfloat16)
        shifted_imag = (spec_real * shift_imag + spec_imag * shift_real).astype(jnp.bfloat16)
        from_real = dot(inverse, shifted_real)
        from_imag = dot(inverse, shifted_imag)
        back[:tile_size, part] = (from_real[:tile_size] - from_imag[tile_size:]).astype(jnp.bfloat16)
        back[tile_size:, part] = (from_imag[:tile_size] + from_real[tile_size:]).astype(jnp.bfloat16)
    for at in range(0, size, width):
        part = slice(at, at + width)
        by_cos = dot(back[...], cos_ref[:, part])
        by_sin = dot(back[...], sin_ref[:, part])
        field_real = by_cos[:tile_size] - by_sin[tile_size:]
        wave_ref[0, :, part] = field_real.astype(jnp.bfloat16)
        wave_ref[1, :, part] = (by_cos[tile_size:] + by_sin[:tile_size]).astype(jnp.bfloat16)
        image_ref[part, :] = (field_real * (1.0 / math.sqrt(slots))).T.astype(jnp.bfloat16)


def whole(memory=pltpu.VMEM):
    return pl.BlockSpec(memory_space=memory)


def exchange(x, axes):
    return lax.all_to_all(x, axes, split_axis=0, concat_axis=0, tiled=True)


def local(wavefield, slowness, freq_ids, depth_owner):
    owner = depth_owner[0]
    swap = [(0, 1), (1, 0)]
    side = lax.axis_index("h").astype(jnp.int32)
    tile = 2 * side + lax.axis_index("c").astype(jnp.int32)
    wavefield = wavefield.reshape(2, slots // 2, 8, tile_size)
    pieces = exchange(slowness.reshape(16, 8, size), ("v", "w", "z"))
    other = lax.ppermute(wavefield, "h", swap)
    pieces = pl.pallas_call(
        pick_kernel,
        out_shape=jax.ShapeDtypeStruct((32, 8, tile_size), jnp.bfloat16),
        in_specs=[whole(pltpu.SMEM), whole()],
        out_specs=whole(),
        compiler_params=pltpu.CompilerParams(vmem_limit_bytes=8 << 20),
        cost_estimate=pl.CostEstimate(flops=10_000, bytes_accessed=100_000, transcendentals=0),
    )(depth_owner, pieces)
    pieces = exchange(pieces, ("u", "l", "h", "c"))
    half = jax.ShapeDtypeStruct((2, slots // 2, 8, tile_size), jnp.bfloat16)
    own, other, factors = pl.pallas_call(
        pack_kernel,
        out_shape=(half, half, jax.ShapeDtypeStruct((slots // 2, 8, tile_size), jnp.float32)),
        in_specs=[whole(pltpu.SMEM)] + [whole()] * 2,
        out_specs=(whole(), whole(), whole()),
        compiler_params=pltpu.CompilerParams(vmem_limit_bytes=8 << 20),
        cost_estimate=pl.CostEstimate(flops=300_000, bytes_accessed=1_300_000, transcendentals=0),
    )(freq_ids, wavefield, other)
    place = (owner // 32 * 2 + owner % 2) * 4 + lax.axis_index("u").astype(jnp.int32)
    lensed = pl.pallas_call(
        lens_kernel,
        out_shape=jax.ShapeDtypeStruct((slots, 8, 2 * tile_size), jnp.bfloat16),
        in_specs=[whole(pltpu.SMEM)] + [whole()] * 4,
        out_specs=whole(),
        compiler_params=pltpu.CompilerParams(vmem_limit_bytes=8 << 20),
        cost_estimate=pl.CostEstimate(flops=6_000_000, bytes_accessed=1_300_000, transcendentals=0),
    )(jnp.stack([place, side]), pieces, own, other, factors)
    columns = exchange(lensed, freq)

    table_cos, table_sin = dft_table(size)
    shift = pl.pallas_call(
        shift_kernel,
        out_shape=jax.ShapeDtypeStruct((2, size, size), jnp.bfloat16),
        in_specs=[whole(pltpu.SMEM)] * 2,
        out_specs=whole(),
        compiler_params=pltpu.CompilerParams(vmem_limit_bytes=16 << 20),
        cost_estimate=pl.CostEstimate(flops=10_000_000, bytes_accessed=2_100_000, transcendentals=500_000),
    )(lax.axis_index(freq).astype(jnp.int32)[None], freq_ids)
    columns, shift = lax.optimization_barrier((columns, shift))

    table_cos, table_sin = jnp.asarray(table_cos), jnp.asarray(table_sin)
    own = pl.pallas_call(
        column_kernel,
        out_shape=jax.ShapeDtypeStruct((2, 2, size, tile_size), jnp.bfloat16),
        in_specs=[whole()] * 3,
        out_specs=whole(),
        scratch_shapes=[pltpu.VMEM((size, 4 * tile_size), jnp.bfloat16)],
        compiler_params=pltpu.CompilerParams(vmem_limit_bytes=8 << 20),
        cost_estimate=pl.CostEstimate(flops=540_000_000, bytes_accessed=2_100_000, transcendentals=0),
    )(table_cos, table_sin, columns)
    beside = lax.ppermute(own, "c", swap)
    wave_next, parts = pl.pallas_call(
        step_kernel,
        out_shape=(
            jax.ShapeDtypeStruct((2, tile_size, size), jnp.bfloat16),
            jax.ShapeDtypeStruct((size, tile_size), jnp.bfloat16),
        ),
        in_specs=[whole(pltpu.SMEM)] + [whole()] * 5,
        out_specs=(whole(), whole()),
        scratch_shapes=[
            pltpu.VMEM((2, size, size), jnp.bfloat16),
            pltpu.VMEM((2 * tile_size, size), jnp.bfloat16),
        ],
        compiler_params=pltpu.CompilerParams(vmem_limit_bytes=20 << 20),
        cost_estimate=pl.CostEstimate(flops=1_620_000_000, bytes_accessed=4_600_000, transcendentals=0),
    )(tile[None], own, beside, table_cos, table_sin, shift)
    parts = exchange(parts.reshape(slots, size // slots, tile_size), freq)
    image = jnp.sum(parts.astype(jnp.float32), axis=0).T
    return (wave_next[:, None], image)


def solution(mesh):
    grid = Mesh(mesh.devices.reshape(4, 2, 2, 4, 2, 2, 2), freq + ("h", "c"))
    tile = ("h", "c")
    return jax.shard_map(
        local,
        mesh=grid,
        in_specs=(P(None, None, freq, tile), P(freq, tile, None), P(), P()),
        out_specs=(P(None, freq, tile, None), P(tile, freq)),
        check_vma=False,
    )
```

```python
import math

import jax
import jax.numpy as jnp
import numpy as np
from jax import lax
from jax.experimental import pallas as pl
from jax.experimental.pallas import tpu as pltpu
from jax.sharding import Mesh
from jax.sharding import PartitionSpec as P

depth_step = 0.5
omega_top = 2.8
slots = 128
size = 512
tile_size = 128
freq = ("u", "v", "w", "z", "l")


def dft_table(length):
    places = np.arange(length)
    angles = 2.0 * np.pi / length * (places[:, None] * places[None, :] % length)
    factor = 1.0 / math.sqrt(length)
    return (
        (np.cos(angles) * factor).astype(jnp.bfloat16),
        (np.sin(angles) * factor).astype(jnp.bfloat16),
    )


def dot(left, right):
    return jnp.dot(left, right, preferred_element_type=jnp.float32)


def series(square, first, last):
    total = (-1.0) ** ((last - first) // 2) / math.factorial(last)
    for order in range(last - 2, first - 1, -2):
        total = (-1.0) ** ((order - first) // 2) / math.factorial(order) + square * total
    return total


def pick_kernel(owner_ref, rows_ref, out_ref):
    source = owner_ref[0] // 2 % 16
    for core in range(2):
        low, high = (rows_ref[source, core, half].astype(jnp.float32) for half in range(2))
        for l in range(2):
            piece = jnp.concatenate([low[4 * l : 4 * l + 4], high[4 * l : 4 * l + 4]], axis=0).astype(jnp.bfloat16)
            for u in (core, core + 2):
                for h in range(2):
                    out_ref[(u * 2 + l) * 2 + h] = piece


def shift_kernel(slot_ref, ids_ref, shift_ref):
    angular = omega_top * (ids_ref[slot_ref[0]] + 1).astype(jnp.float32) / slots

    def square(start, shape, axis):
        places = lax.broadcasted_iota(jnp.int32, shape, axis) + start
        signed = jnp.where(places < size // 2, places, places - size)
        return (2.0 * math.pi / size * signed.astype(jnp.float32)) ** 2

    ky_square = square(0, (16, size), 1)

    @pl.loop(0, size, step=16)
    def _(start):
        start = pl.multiple_of(start, 16)
        vertical = angular * angular - square(start, (16, size), 0) - ky_square
        root = depth_step * jnp.sqrt(jnp.abs(vertical))
        travel = jnp.where(vertical > 0.0, root, 0.0)
        damping = jnp.exp(jnp.where(vertical < 0.0, -root, 0.0))
        travel_square = travel * travel
        shift_ref[0, pl.ds(start, 16), :] = (damping * series(travel_square, 0, 12)).astype(jnp.bfloat16)
        shift_ref[1, pl.ds(start, 16), :] = (damping * travel * series(travel_square, 1, 13)).astype(jnp.bfloat16)


def pack_kernel(own_ref, other_ref, wave_ref):
    for slot in range(slots):
        for part in range(2):
            both = jnp.concatenate([own_ref[part, slot].astype(jnp.float32), other_ref[part, slot].astype(jnp.float32)], axis=0)
            wave_ref[slot, part] = both.astype(jnp.bfloat16)


def lens_kernel(place_ref, slow_ref, wave_ref, out_ref, turn):
    slow = slow_ref[place_ref[0]].astype(jnp.float32)
    swapped = jnp.concatenate([slow[4:], slow[:4]], axis=0)
    unit = (depth_step * omega_top / slots) * (jnp.where(place_ref[1] == 0, slow, swapped) - 1.0)

    def turned(count):
        phase = unit * float(count)
        square = phase * phase
        return series(square, 0, 8), phase * series(square, 1, 9)

    fine = [turned(count) for count in range(1, 17)]
    for group in range(slots // 16):
        group_cos, group_sin = turned(16 * group)
        for at, (fine_cos, fine_sin) in enumerate(fine):
            turn[16 * group + at, 0] = group_cos * fine_cos - group_sin * fine_sin
            turn[16 * group + at, 1] = group_cos * fine_sin + group_sin * fine_cos
    for slot in range(slots):
        number = place_ref[2 + slot]
        lens_cos, lens_sin = turn[number, 0], turn[number, 1]
        wave_real = wave_ref[slot, 0].astype(jnp.float32)
        wave_imag = wave_ref[slot, 1].astype(jnp.float32)
        real = wave_real * lens_cos - wave_imag * lens_sin
        imag = wave_real * lens_sin + wave_imag * lens_cos
        out_ref[slot, :, :tile_size] = jnp.concatenate([real[:4], imag[:4]], axis=0).astype(jnp.bfloat16)
        out_ref[slot, :, tile_size:] = jnp.concatenate([real[4:], imag[4:]], axis=0).astype(jnp.bfloat16)


def column_kernel(cos_ref, sin_ref, wave_ref, out_ref, both):
    for at in range(0, size // 4, 4):
        tiles = [wave_ref[at + k].astype(jnp.float32) for k in range(4)]
        for part in range(2):
            rows = jnp.concatenate([tile[4 * part : 4 * part + 4] for tile in tiles], axis=0)
            both[4 * at : 4 * at + 16, part * 2 * tile_size : (part + 1) * 2 * tile_size] = rows.astype(jnp.bfloat16)
    by_cos = dot(cos_ref[...], both[...])
    by_sin = dot(sin_ref[...], both[...])
    real = (by_cos[:, : 2 * tile_size] + by_sin[:, 2 * tile_size :]).astype(jnp.bfloat16)
    imag = (by_cos[:, 2 * tile_size :] - by_sin[:, : 2 * tile_size]).astype(jnp.bfloat16)
    for block in range(2):
        lanes = slice(block * tile_size, (block + 1) * tile_size)
        out_ref[block, 0] = real[:, lanes]
        out_ref[block, 1] = imag[:, lanes]


def step_kernel(tile_ref, own_ref, other_ref, cos_ref, sin_ref, shift_ref, wave_ref, image_ref, field, back):
    tile = tile_ref[0]
    for flip in range(4):
        block = (own_ref, other_ref)[flip % 2]
        start = pl.multiple_of((tile ^ flip) * tile_size, tile_size)
        field[:, :, pl.ds(start, tile_size)] = block[flip // 2]
    rows = pl.ds(pl.multiple_of(tile * tile_size, tile_size), tile_size)
    inverse = jnp.concatenate([cos_ref[rows, :], sin_ref[rows, :]], axis=0)
    width = 256
    for at in range(0, size, width):
        part = slice(at, at + width)
        spec_real = dot(field[0], cos_ref[:, part]) + dot(field[1], sin_ref[:, part])
        spec_imag = dot(field[1], cos_ref[:, part]) - dot(field[0], sin_ref[:, part])
        shift_real = shift_ref[0, :, part].astype(jnp.float32)
        shift_imag = shift_ref[1, :, part].astype(jnp.float32)
        shifted_real = (spec_real * shift_real - spec_imag * shift_imag).astype(jnp.bfloat16)
        shifted_imag = (spec_real * shift_imag + spec_imag * shift_real).astype(jnp.bfloat16)
        from_real = dot(inverse, shifted_real)
        from_imag = dot(inverse, shifted_imag)
        back[:tile_size, part] = (from_real[:tile_size] - from_imag[tile_size:]).astype(jnp.bfloat16)
        back[tile_size:, part] = (from_imag[:tile_size] + from_real[tile_size:]).astype(jnp.bfloat16)
    for at in range(0, size, width):
        part = slice(at, at + width)
        by_cos = dot(back[...], cos_ref[:, part])
        by_sin = dot(back[...], sin_ref[:, part])
        field_real = by_cos[:tile_size] - by_sin[tile_size:]
        wave_ref[0, :, part] = field_real.astype(jnp.bfloat16)
        wave_ref[1, :, part] = (by_cos[tile_size:] + by_sin[:tile_size]).astype(jnp.bfloat16)
        image_ref[part, :] = (field_real * (1.0 / math.sqrt(slots))).T.astype(jnp.bfloat16)


def whole(memory=pltpu.VMEM):
    return pl.BlockSpec(memory_space=memory)


def exchange(x, axes):
    return lax.all_to_all(x, axes, split_axis=0, concat_axis=0, tiled=True)


def local(wavefield, slowness, freq_ids, depth_owner):
    owner = depth_owner[0]
    swap = [(0, 1), (1, 0)]
    side = lax.axis_index("h").astype(jnp.int32)
    tile = 2 * side + lax.axis_index("c").astype(jnp.int32)
    pieces = slowness.reshape(16, 8, 2, 2, tile_size).transpose(0, 3, 2, 1, 4)
    pieces = exchange(pieces.reshape(32, 2, 8, tile_size), ("v", "w", "z", "c"))
    other = lax.ppermute(wavefield, "h", swap)
    pieces = pl.pallas_call(
        pick_kernel,
        out_shape=jax.ShapeDtypeStruct((16, 8, tile_size), jnp.bfloat16),
        in_specs=[whole(pltpu.SMEM), whole()],
        out_specs=whole(),
        compiler_params=pltpu.CompilerParams(vmem_limit_bytes=8 << 20),
        cost_estimate=pl.CostEstimate(flops=10_000, bytes_accessed=100_000, transcendentals=0),
    )(depth_owner, pieces.reshape(16, 2, 2, 8, tile_size))
    pieces = exchange(pieces, ("u", "l", "h"))
    waves = pl.pallas_call(
        pack_kernel,
        out_shape=jax.ShapeDtypeStruct((slots, 2, 8, tile_size), jnp.bfloat16),
        in_specs=[whole()] * 2,
        out_specs=whole(),
        compiler_params=pltpu.CompilerParams(vmem_limit_bytes=8 << 20),
        cost_estimate=pl.CostEstimate(flops=300_000, bytes_accessed=1_000_000, transcendentals=0),
    )(wavefield, other)
    place = (owner // 32 * 2 + owner % 2) * 2 + lax.axis_index("u").astype(jnp.int32) // 2
    lensed = pl.pallas_call(
        lens_kernel,
        out_shape=jax.ShapeDtypeStruct((slots, 8, 2 * tile_size), jnp.bfloat16),
        in_specs=[whole(pltpu.SMEM)] + [whole()] * 2,
        out_specs=whole(),
        scratch_shapes=[pltpu.VMEM((slots, 2, 8, tile_size), jnp.float32)],
        compiler_params=pltpu.CompilerParams(vmem_limit_bytes=8 << 20),
        cost_estimate=pl.CostEstimate(flops=3_000_000, bytes_accessed=1_100_000, transcendentals=0),
    )(jnp.concatenate([jnp.stack([place, side]), freq_ids]), pieces, waves)
    columns = exchange(lensed, freq)

    table_cos, table_sin = dft_table(size)
    shift = pl.pallas_call(
        shift_kernel,
        out_shape=jax.ShapeDtypeStruct((2, size, size), jnp.bfloat16),
        in_specs=[whole(pltpu.SMEM)] * 2,
        out_specs=whole(),
        compiler_params=pltpu.CompilerParams(vmem_limit_bytes=16 << 20),
        cost_estimate=pl.CostEstimate(flops=10_000_000, bytes_accessed=2_100_000, transcendentals=500_000),
    )(lax.axis_index(freq).astype(jnp.int32)[None], freq_ids)
    columns, shift = lax.optimization_barrier((columns, shift))

    table_cos, table_sin = jnp.asarray(table_cos), jnp.asarray(table_sin)
    own = pl.pallas_call(
        column_kernel,
        out_shape=jax.ShapeDtypeStruct((2, 2, size, tile_size), jnp.bfloat16),
        in_specs=[whole()] * 3,
        out_specs=whole(),
        scratch_shapes=[pltpu.VMEM((size, 4 * tile_size), jnp.bfloat16)],
        compiler_params=pltpu.CompilerParams(vmem_limit_bytes=8 << 20),
        cost_estimate=pl.CostEstimate(flops=540_000_000, bytes_accessed=2_100_000, transcendentals=0),
    )(table_cos, table_sin, columns)
    beside = lax.ppermute(own, "c", swap)
    wave_next, parts = pl.pallas_call(
        step_kernel,
        out_shape=(
            jax.ShapeDtypeStruct((2, tile_size, size), jnp.bfloat16),
            jax.ShapeDtypeStruct((size, tile_size), jnp.bfloat16),
        ),
        in_specs=[whole(pltpu.SMEM)] + [whole()] * 5,
        out_specs=(whole(), whole()),
        scratch_shapes=[
            pltpu.VMEM((2, size, size), jnp.bfloat16),
            pltpu.VMEM((2 * tile_size, size), jnp.bfloat16),
        ],
        compiler_params=pltpu.CompilerParams(vmem_limit_bytes=20 << 20),
        cost_estimate=pl.CostEstimate(flops=1_620_000_000, bytes_accessed=4_600_000, transcendentals=0),
    )(tile[None], own, beside, table_cos, table_sin, shift)
    parts = exchange(parts.reshape(slots, size // slots, tile_size), freq)
    image = jnp.sum(parts.astype(jnp.float32), axis=0).T
    return (wave_next[:, None], image)


def solution(mesh):
    grid = Mesh(mesh.devices.reshape(4, 2, 2, 4, 2, 2, 2), freq + ("h", "c"))
    tile = ("h", "c")
    return jax.shard_map(
        local,
        mesh=grid,
        in_specs=(P(None, None, freq, tile), P(freq, tile, None), P(), P()),
        out_specs=(P(None, freq, tile, None), P(tile, freq)),
        check_vma=False,
    )
```

```python
import math

import jax
import jax.numpy as jnp
import numpy as np
from jax import lax
from jax.experimental import pallas as pl
from jax.experimental.pallas import tpu as pltpu
from jax.sharding import Mesh
from jax.sharding import PartitionSpec as P

depth_step = 0.5
omega_top = 2.8
slots = 128
size = 512
tile_size = 128
freq = ("y4", "y2", "y1", "w", "z4", "z2", "z1")
mixed = ("z1", "y1", "w", "z2", "y2", "z4", "y4")


def place_of(slot):
    bits = {axis: slot >> (len(freq) - 1 - at) & 1 for at, axis in enumerate(freq)}
    return sum(bits[axis] << (len(mixed) - 1 - at) for at, axis in enumerate(mixed))


def dft_table(length):
    places = np.arange(length)
    angles = 2.0 * np.pi / length * (places[:, None] * places[None, :] % length)
    factor = 1.0 / math.sqrt(length)
    return (
        (np.cos(angles) * factor).astype(jnp.bfloat16),
        (np.sin(angles) * factor).astype(jnp.bfloat16),
    )


def dot(left, right):
    return jnp.dot(left, right, preferred_element_type=jnp.float32)


def series(square, first, last):
    total = (-1.0) ** ((last - first) // 2) / math.factorial(last)
    for order in range(last - 2, first - 1, -2):
        total = (-1.0) ** ((order - first) // 2) / math.factorial(order) + square * total
    return total


def pick_kernel(owner_ref, rows_ref, out_ref):
    rows = rows_ref[owner_ref[0] // 2 % 16].astype(jnp.float32)
    for l in range(2):
        for c in range(2):
            lanes = (c * tile_size, (2 + c) * tile_size)
            piece = jnp.concatenate([rows[4 * l : 4 * l + 4, lane : lane + tile_size] for lane in lanes], axis=0)
            piece = piece.astype(jnp.bfloat16)
            for u in range(4):
                for h in range(2):
                    out_ref[((u * 2 + l) * 2 + h) * 2 + c] = piece


def shift_kernel(slot_ref, ids_ref, shift_ref):
    angular = omega_top * (ids_ref[slot_ref[0]] + 1).astype(jnp.float32) / slots

    def square(start, shape, axis):
        places = lax.broadcasted_iota(jnp.int32, shape, axis) + start
        signed = jnp.where(places < size // 2, places, places - size)
        return (2.0 * math.pi / size * signed.astype(jnp.float32)) ** 2

    ky_square = square(0, (16, size), 1)

    @pl.loop(0, size, step=16)
    def _(start):
        start = pl.multiple_of(start, 16)
        vertical = angular * angular - square(start, (16, size), 0) - ky_square
        root = depth_step * jnp.sqrt(jnp.abs(vertical))
        travel = jnp.where(vertical > 0.0, root, 0.0)
        damping = jnp.exp(jnp.where(vertical < 0.0, -root, 0.0))
        travel_square = travel * travel
        shift_ref[0, pl.ds(start, 16), :] = (damping * series(travel_square, 0, 12)).astype(jnp.bfloat16)
        shift_ref[1, pl.ds(start, 16), :] = (damping * travel * series(travel_square, 1, 13)).astype(jnp.bfloat16)


def pack_kernel(ids_ref, own_ref, other_ref, own_out, other_out, factor_ref):
    own_out[...] = own_ref[...]
    other_out[...] = other_ref[...]
    first = lax.broadcasted_iota(jnp.int32, (8, tile_size), 0) < 4
    for pair in range(slots // 2):
        low, high = (
            depth_step * (omega_top * (ids_ref[2 * pair + at] + 1).astype(jnp.float32) / slots) for at in range(2)
        )
        factor_ref[pair] = jnp.where(first, low, high)


def lens_kernel(place_ref, slow_ref, own_ref, other_ref, factor_ref, out_ref):
    slow = slow_ref[place_ref[0]].astype(jnp.float32) - 1.0
    halves = (jnp.concatenate([slow[:4]] * 2, axis=0), jnp.concatenate([slow[4:]] * 2, axis=0))
    low = place_ref[1] == 0
    depths = (jnp.where(low, halves[0], halves[1]), jnp.where(low, halves[1], halves[0]))
    for pair in range(slots // 2):
        factor = factor_ref[pair]
        for block, (ref, depth) in enumerate(zip((own_ref, other_ref), depths)):
            phase = factor * depth
            square = phase * phase
            lens_cos = series(square, 0, 8)
            lens_sin = phase * series(square, 1, 9)
            wave_real = ref[0, pair].astype(jnp.float32)
            wave_imag = ref[1, pair].astype(jnp.float32)
            real = wave_real * lens_cos - wave_imag * lens_sin
            imag = wave_real * lens_sin + wave_imag * lens_cos
            lanes = slice(block * tile_size, (block + 1) * tile_size)
            out_ref[place_of(2 * pair), :, lanes] = jnp.concatenate([real[:4], imag[:4]], axis=0).astype(jnp.bfloat16)
            out_ref[place_of(2 * pair + 1), :, lanes] = jnp.concatenate([real[4:], imag[4:]], axis=0).astype(jnp.bfloat16)


def column_kernel(cos_ref, sin_ref, wave_ref, out_ref, both):
    for at in range(0, size // 4, 4):
        tiles = [wave_ref[place_of(at + k)].astype(jnp.float32) for k in range(4)]
        for part in range(2):
            rows = jnp.concatenate([tile[4 * part : 4 * part + 4] for tile in tiles], axis=0)
            both[4 * at : 4 * at + 16, part * 2 * tile_size : (part + 1) * 2 * tile_size] = rows.astype(jnp.bfloat16)
    by_cos = dot(cos_ref[...], both[...])
    by_sin = dot(sin_ref[...], both[...])
    real = (by_cos[:, : 2 * tile_size] + by_sin[:, 2 * tile_size :]).astype(jnp.bfloat16)
    imag = (by_cos[:, 2 * tile_size :] - by_sin[:, : 2 * tile_size]).astype(jnp.bfloat16)
    for block in range(2):
        lanes = slice(block * tile_size, (block + 1) * tile_size)
        out_ref[block, 0] = real[:, lanes]
        out_ref[block, 1] = imag[:, lanes]


def step_kernel(tile_ref, own_ref, other_ref, cos_ref, sin_ref, shift_ref, wave_ref, image_ref, field, back):
    tile = tile_ref[0]
    for flip in range(4):
        block = (own_ref, other_ref)[flip % 2]
        start = pl.multiple_of((tile ^ flip) * tile_size, tile_size)
        field[:, :, pl.ds(start, tile_size)] = block[flip // 2]
    rows = pl.ds(pl.multiple_of(tile * tile_size, tile_size), tile_size)
    inverse = jnp.concatenate([cos_ref[rows, :], sin_ref[rows, :]], axis=0)
    width = 256
    for at in range(0, size, width):
        part = slice(at, at + width)
        spec_real = dot(field[0], cos_ref[:, part]) + dot(field[1], sin_ref[:, part])
        spec_imag = dot(field[1], cos_ref[:, part]) - dot(field[0], sin_ref[:, part])
        shift_real = shift_ref[0, :, part].astype(jnp.float32)
        shift_imag = shift_ref[1, :, part].astype(jnp.float32)
        shifted_real = (spec_real * shift_real - spec_imag * shift_imag).astype(jnp.bfloat16)
        shifted_imag = (spec_real * shift_imag + spec_imag * shift_real).astype(jnp.bfloat16)
        from_real = dot(inverse, shifted_real)
        from_imag = dot(inverse, shifted_imag)
        back[:tile_size, part] = (from_real[:tile_size] - from_imag[tile_size:]).astype(jnp.bfloat16)
        back[tile_size:, part] = (from_imag[:tile_size] + from_real[tile_size:]).astype(jnp.bfloat16)
    for at in range(0, size, width):
        part = slice(at, at + width)
        by_cos = dot(back[...], cos_ref[:, part])
        by_sin = dot(back[...], sin_ref[:, part])
        field_real = by_cos[:tile_size] - by_sin[tile_size:]
        wave_ref[0, :, part] = field_real.astype(jnp.bfloat16)
        wave_ref[1, :, part] = (by_cos[tile_size:] + by_sin[:tile_size]).astype(jnp.bfloat16)
        image = (field_real * (1.0 / math.sqrt(slots))).T.astype(jnp.bfloat16)
        for slot in range(at // 4, (at + width) // 4):
            image_ref[place_of(slot)] = image[4 * slot - at : 4 * slot - at + 4]


def whole(memory=pltpu.VMEM):
    return pl.BlockSpec(memory_space=memory)


def exchange(x, axes):
    return lax.all_to_all(x, axes, split_axis=0, concat_axis=0, tiled=True)


def local(wavefield, slowness, freq_ids, depth_owner):
    owner = depth_owner[0]
    swap = [(0, 1), (1, 0)]
    side = lax.axis_index("h").astype(jnp.int32)
    tile = 2 * side + lax.axis_index("c").astype(jnp.int32)
    wavefield = wavefield.reshape(2, slots // 2, 8, tile_size)
    pieces = exchange(slowness.reshape(16, 8, size), ("y1", "w", "z4", "z2"))
    other = lax.ppermute(wavefield, "h", swap)
    pieces = pl.pallas_call(
        pick_kernel,
        out_shape=jax.ShapeDtypeStruct((32, 8, tile_size), jnp.bfloat16),
        in_specs=[whole(pltpu.SMEM), whole()],
        out_specs=whole(),
        compiler_params=pltpu.CompilerParams(vmem_limit_bytes=8 << 20),
        cost_estimate=pl.CostEstimate(flops=10_000, bytes_accessed=100_000, transcendentals=0),
    )(depth_owner, pieces)
    pieces = exchange(pieces, ("y4", "y2", "z1", "h", "c"))
    half = jax.ShapeDtypeStruct((2, slots // 2, 8, tile_size), jnp.bfloat16)
    own, other, factors = pl.pallas_call(
        pack_kernel,
        out_shape=(half, half, jax.ShapeDtypeStruct((slots // 2, 8, tile_size), jnp.float32)),
        in_specs=[whole(pltpu.SMEM)] + [whole()] * 2,
        out_specs=(whole(), whole(), whole()),
        compiler_params=pltpu.CompilerParams(vmem_limit_bytes=8 << 20),
        cost_estimate=pl.CostEstimate(flops=300_000, bytes_accessed=1_300_000, transcendentals=0),
    )(freq_ids, wavefield, other)
    place = (owner // 32 * 2 + owner % 2) * 4 + lax.axis_index(("y4", "y2")).astype(jnp.int32)
    lensed = pl.pallas_call(
        lens_kernel,
        out_shape=jax.ShapeDtypeStruct((slots, 8, 2 * tile_size), jnp.bfloat16),
        in_specs=[whole(pltpu.SMEM)] + [whole()] * 4,
        out_specs=whole(),
        compiler_params=pltpu.CompilerParams(vmem_limit_bytes=8 << 20),
        cost_estimate=pl.CostEstimate(flops=6_000_000, bytes_accessed=1_300_000, transcendentals=0),
    )(jnp.stack([place, side]), pieces, own, other, factors)
    columns = exchange(lensed, mixed)

    table_cos, table_sin = dft_table(size)
    shift = pl.pallas_call(
        shift_kernel,
        out_shape=jax.ShapeDtypeStruct((2, size, size), jnp.bfloat16),
        in_specs=[whole(pltpu.SMEM)] * 2,
        out_specs=whole(),
        compiler_params=pltpu.CompilerParams(vmem_limit_bytes=16 << 20),
        cost_estimate=pl.CostEstimate(flops=10_000_000, bytes_accessed=2_100_000, transcendentals=500_000),
    )(lax.axis_index(freq).astype(jnp.int32)[None], freq_ids)
    columns, shift = lax.optimization_barrier((columns, shift))

    table_cos, table_sin = jnp.asarray(table_cos), jnp.asarray(table_sin)
    own = pl.pallas_call(
        column_kernel,
        out_shape=jax.ShapeDtypeStruct((2, 2, size, tile_size), jnp.bfloat16),
        in_specs=[whole()] * 3,
        out_specs=whole(),
        scratch_shapes=[pltpu.VMEM((size, 4 * tile_size), jnp.bfloat16)],
        compiler_params=pltpu.CompilerParams(vmem_limit_bytes=8 << 20),
        cost_estimate=pl.CostEstimate(flops=540_000_000, bytes_accessed=2_100_000, transcendentals=0),
    )(table_cos, table_sin, columns)
    beside = lax.ppermute(own, "c", swap)
    wave_next, parts = pl.pallas_call(
        step_kernel,
        out_shape=(
            jax.ShapeDtypeStruct((2, tile_size, size), jnp.bfloat16),
            jax.ShapeDtypeStruct((slots, size // slots, tile_size), jnp.bfloat16),
        ),
        in_specs=[whole(pltpu.SMEM)] + [whole()] * 5,
        out_specs=(whole(), whole()),
        scratch_shapes=[
            pltpu.VMEM((2, size, size), jnp.bfloat16),
            pltpu.VMEM((2 * tile_size, size), jnp.bfloat16),
        ],
        compiler_params=pltpu.CompilerParams(vmem_limit_bytes=20 << 20),
        cost_estimate=pl.CostEstimate(flops=1_620_000_000, bytes_accessed=4_600_000, transcendentals=0),
    )(tile[None], own, beside, table_cos, table_sin, shift)
    parts = exchange(parts, mixed)
    image = jnp.sum(parts.astype(jnp.float32), axis=0).T
    return (wave_next[:, None], image)


def solution(mesh):
    grid = Mesh(mesh.devices.reshape((2,) * 9), freq + ("h", "c"))
    tile = ("h", "c")
    return jax.shard_map(
        local,
        mesh=grid,
        in_specs=(P(None, None, freq, tile), P(freq, tile, None), P(), P()),
        out_specs=(P(None, freq, tile, None), P(tile, freq)),
        check_vma=False,
    )
```

```python
import math

import jax
import jax.numpy as jnp
import numpy as np
from jax import lax
from jax.experimental import pallas as pl
from jax.experimental.pallas import tpu as pltpu
from jax.sharding import Mesh
from jax.sharding import PartitionSpec as P

depth_step = 0.5
omega_top = 2.8
slots = 128
size = 512
tile_size = 128
freq = ("u", "v", "w", "z", "l")


def dft_table(length):
    places = np.arange(length)
    angles = 2.0 * np.pi / length * (places[:, None] * places[None, :] % length)
    factor = 1.0 / math.sqrt(length)
    return (
        (np.cos(angles) * factor).astype(jnp.bfloat16),
        (np.sin(angles) * factor).astype(jnp.bfloat16),
    )


def dot(left, right):
    return jnp.dot(left, right, preferred_element_type=jnp.float32)


def series(square, first, last):
    total = (-1.0) ** ((last - first) // 2) / math.factorial(last)
    for order in range(last - 2, first - 1, -2):
        total = (-1.0) ** ((order - first) // 2) / math.factorial(order) + square * total
    return total


def scatter_kernel(slow_ref, out_ref):
    for at in range(0, 32, 4):
        slow = slow_ref[0, 4 * at : 4 * at + 16, :].astype(jnp.float32)
        for c in range(2):
            for k in range(4):
                rows = slow[4 * k : 4 * k + 4]
                pieces = [rows[:, lane : lane + tile_size] for lane in (c * tile_size, (2 + c) * tile_size)]
                piece = jnp.concatenate(pieces, axis=0).astype(jnp.bfloat16)
                for h in range(2):
                    out_ref[(at + k) * 4 + h * 2 + c] = piece


def shift_kernel(slot_ref, ids_ref, shift_ref):
    angular = omega_top * (ids_ref[slot_ref[0]] + 1).astype(jnp.float32) / slots

    def square(start, shape, axis):
        places = lax.broadcasted_iota(jnp.int32, shape, axis) + start
        signed = jnp.where(places < size // 2, places, places - size)
        return (2.0 * math.pi / size * signed.astype(jnp.float32)) ** 2

    ky_square = square(0, (16, size), 1)

    @pl.loop(0, size, step=16)
    def _(start):
        start = pl.multiple_of(start, 16)
        vertical = angular * angular - square(start, (16, size), 0) - ky_square
        root = depth_step * jnp.sqrt(jnp.abs(vertical))
        travel = jnp.where(vertical > 0.0, root, 0.0)
        damping = jnp.exp(jnp.where(vertical < 0.0, -root, 0.0))
        travel_square = travel * travel
        shift_ref[0, pl.ds(start, 16), :] = (damping * series(travel_square, 0, 12)).astype(jnp.bfloat16)
        shift_ref[1, pl.ds(start, 16), :] = (damping * travel * series(travel_square, 1, 13)).astype(jnp.bfloat16)


def pack_kernel(ids_ref, own_ref, other_ref, own_out, other_out, factor_ref):
    own_out[...] = own_ref[...]
    other_out[...] = other_ref[...]
    first = lax.broadcasted_iota(jnp.int32, (8, tile_size), 0) < 4
    for pair in range(slots // 2):
        low, high = (
            depth_step * (omega_top * (ids_ref[2 * pair + at] + 1).astype(jnp.float32) / slots) for at in range(2)
        )
        factor_ref[pair] = jnp.where(first, low, high)


def lens_kernel(place_ref, slow_ref, own_ref, other_ref, factor_ref, out_ref):
    slow = slow_ref[place_ref[0]].astype(jnp.float32) - 1.0
    halves = (jnp.concatenate([slow[:4]] * 2, axis=0), jnp.concatenate([slow[4:]] * 2, axis=0))
    low = place_ref[1] == 0
    depths = (jnp.where(low, halves[0], halves[1]), jnp.where(low, halves[1], halves[0]))
    for pair in range(slots // 2):
        factor = factor_ref[pair]
        for block, (ref, depth) in enumerate(zip((own_ref, other_ref), depths)):
            phase = factor * depth
            square = phase * phase
            lens_cos = series(square, 0, 8)
            lens_sin = phase * series(square, 1, 9)
            wave_real = ref[0, pair].astype(jnp.float32)
            wave_imag = ref[1, pair].astype(jnp.float32)
            real = wave_real * lens_cos - wave_imag * lens_sin
            imag = wave_real * lens_sin + wave_imag * lens_cos
            both = jnp.concatenate([real[:4], imag[:4], real[4:], imag[4:]], axis=0).astype(jnp.bfloat16)
            out_ref[pair, :, block * tile_size : (block + 1) * tile_size] = both


def column_kernel(cos_ref, sin_ref, wave_ref, out_ref, both):
    for at in range(0, size // 4, 4):
        tiles = [wave_ref[at + k].astype(jnp.float32) for k in range(4)]
        for part in range(2):
            rows = jnp.concatenate([tile[4 * part : 4 * part + 4] for tile in tiles], axis=0)
            both[4 * at : 4 * at + 16, part * 2 * tile_size : (part + 1) * 2 * tile_size] = rows.astype(jnp.bfloat16)
    by_cos = dot(cos_ref[...], both[...])
    by_sin = dot(sin_ref[...], both[...])
    real = (by_cos[:, : 2 * tile_size] + by_sin[:, 2 * tile_size :]).astype(jnp.bfloat16)
    imag = (by_cos[:, 2 * tile_size :] - by_sin[:, : 2 * tile_size]).astype(jnp.bfloat16)
    for block in range(2):
        lanes = slice(block * tile_size, (block + 1) * tile_size)
        out_ref[block, 0] = real[:, lanes]
        out_ref[block, 1] = imag[:, lanes]


def step_kernel(tile_ref, own_ref, other_ref, cos_ref, sin_ref, shift_ref, wave_ref, image_ref, field, back):
    tile = tile_ref[0]
    for flip in range(4):
        block = (own_ref, other_ref)[flip % 2]
        start = pl.multiple_of((tile ^ flip) * tile_size, tile_size)
        field[:, :, pl.ds(start, tile_size)] = block[flip // 2]
    rows = pl.ds(pl.multiple_of(tile * tile_size, tile_size), tile_size)
    inverse = jnp.concatenate([cos_ref[rows, :], sin_ref[rows, :]], axis=0)
    width = 256
    for at in range(0, size, width):
        part = slice(at, at + width)
        spec_real = dot(field[0], cos_ref[:, part]) + dot(field[1], sin_ref[:, part])
        spec_imag = dot(field[1], cos_ref[:, part]) - dot(field[0], sin_ref[:, part])
        shift_real = shift_ref[0, :, part].astype(jnp.float32)
        shift_imag = shift_ref[1, :, part].astype(jnp.float32)
        shifted_real = (spec_real * shift_real - spec_imag * shift_imag).astype(jnp.bfloat16)
        shifted_imag = (spec_real * shift_imag + spec_imag * shift_real).astype(jnp.bfloat16)
        from_real = dot(inverse, shifted_real)
        from_imag = dot(inverse, shifted_imag)
        back[:tile_size, part] = (from_real[:tile_size] - from_imag[tile_size:]).astype(jnp.bfloat16)
        back[tile_size:, part] = (from_imag[:tile_size] + from_real[tile_size:]).astype(jnp.bfloat16)
    for at in range(0, size, width):
        part = slice(at, at + width)
        by_cos = dot(back[...], cos_ref[:, part])
        by_sin = dot(back[...], sin_ref[:, part])
        field_real = by_cos[:tile_size] - by_sin[tile_size:]
        wave_ref[0, :, part] = field_real.astype(jnp.bfloat16)
        wave_ref[1, :, part] = (by_cos[tile_size:] + by_sin[:tile_size]).astype(jnp.bfloat16)
        image_ref[part, :] = (field_real * (1.0 / math.sqrt(slots))).T.astype(jnp.bfloat16)


def whole(memory=pltpu.VMEM):
    return pl.BlockSpec(memory_space=memory)


def exchange(x, axes):
    return lax.all_to_all(x, axes, split_axis=0, concat_axis=0, tiled=True)


def local(wavefield, slowness, freq_ids, depth_owner):
    owner = depth_owner[0]
    swap = [(0, 1), (1, 0)]
    side = lax.axis_index("h").astype(jnp.int32)
    tile = 2 * side + lax.axis_index("c").astype(jnp.int32)
    wavefield = wavefield.reshape(2, slots // 2, 8, tile_size)
    pieces = pl.pallas_call(
        scatter_kernel,
        out_shape=jax.ShapeDtypeStruct((slots, 8, tile_size), jnp.bfloat16),
        in_specs=[whole()],
        out_specs=whole(),
        compiler_params=pltpu.CompilerParams(vmem_limit_bytes=8 << 20),
        cost_estimate=pl.CostEstimate(flops=10_000, bytes_accessed=400_000, transcendentals=0),
    )(slowness)
    pieces = exchange(pieces, ("v", "w", "z", "l", "h", "c")).reshape(32, 4, 8, tile_size)
    other = lax.ppermute(wavefield, "h", swap)
    pieces = lax.dynamic_index_in_dim(pieces, owner % 32, 0, keepdims=False)
    pieces = exchange(pieces, "u")
    half = jax.ShapeDtypeStruct((2, slots // 2, 8, tile_size), jnp.bfloat16)
    own, other, factors = pl.pallas_call(
        pack_kernel,
        out_shape=(half, half, jax.ShapeDtypeStruct((slots // 2, 8, tile_size), jnp.float32)),
        in_specs=[whole(pltpu.SMEM)] + [whole()] * 2,
        out_specs=(whole(), whole(), whole()),
        compiler_params=pltpu.CompilerParams(vmem_limit_bytes=8 << 20),
        cost_estimate=pl.CostEstimate(flops=300_000, bytes_accessed=1_300_000, transcendentals=0),
    )(freq_ids, wavefield, other)
    place = owner // 32
    lensed = pl.pallas_call(
        lens_kernel,
        out_shape=jax.ShapeDtypeStruct((slots // 2, 16, 2 * tile_size), jnp.bfloat16),
        in_specs=[whole(pltpu.SMEM)] + [whole()] * 4,
        out_specs=whole(),
        compiler_params=pltpu.CompilerParams(vmem_limit_bytes=8 << 20),
        cost_estimate=pl.CostEstimate(flops=6_000_000, bytes_accessed=1_300_000, transcendentals=0),
    )(jnp.stack([place, side]), pieces, own, other, factors)
    columns = exchange(lensed.reshape(slots, 8, 2 * tile_size), freq)

    table_cos, table_sin = dft_table(size)
    shift = pl.pallas_call(
        shift_kernel,
        out_shape=jax.ShapeDtypeStruct((2, size, size), jnp.bfloat16),
        in_specs=[whole(pltpu.SMEM)] * 2,
        out_specs=whole(),
        compiler_params=pltpu.CompilerParams(vmem_limit_bytes=16 << 20),
        cost_estimate=pl.CostEstimate(flops=10_000_000, bytes_accessed=2_100_000, transcendentals=500_000),
    )(lax.axis_index(freq).astype(jnp.int32)[None], freq_ids)
    columns, shift = lax.optimization_barrier((columns, shift))

    table_cos, table_sin = jnp.asarray(table_cos), jnp.asarray(table_sin)
    own = pl.pallas_call(
        column_kernel,
        out_shape=jax.ShapeDtypeStruct((2, 2, size, tile_size), jnp.bfloat16),
        in_specs=[whole()] * 3,
        out_specs=whole(),
        scratch_shapes=[pltpu.VMEM((size, 4 * tile_size), jnp.bfloat16)],
        compiler_params=pltpu.CompilerParams(vmem_limit_bytes=8 << 20),
        cost_estimate=pl.CostEstimate(flops=540_000_000, bytes_accessed=2_100_000, transcendentals=0),
    )(table_cos, table_sin, columns)
    beside = lax.ppermute(own, "c", swap)
    wave_next, parts = pl.pallas_call(
        step_kernel,
        out_shape=(
            jax.ShapeDtypeStruct((2, tile_size, size), jnp.bfloat16),
            jax.ShapeDtypeStruct((size, tile_size), jnp.bfloat16),
        ),
        in_specs=[whole(pltpu.SMEM)] + [whole()] * 5,
        out_specs=(whole(), whole()),
        scratch_shapes=[
            pltpu.VMEM((2, size, size), jnp.bfloat16),
            pltpu.VMEM((2 * tile_size, size), jnp.bfloat16),
        ],
        compiler_params=pltpu.CompilerParams(vmem_limit_bytes=20 << 20),
        cost_estimate=pl.CostEstimate(flops=1_620_000_000, bytes_accessed=4_600_000, transcendentals=0),
    )(tile[None], own, beside, table_cos, table_sin, shift)
    parts = exchange(parts.reshape(slots, size // slots, tile_size), freq)
    image = jnp.sum(parts.astype(jnp.float32), axis=0).T
    return (wave_next[:, None], image)


def solution(mesh):
    grid = Mesh(mesh.devices.reshape(4, 2, 2, 4, 2, 2, 2), freq + ("h", "c"))
    tile = ("h", "c")
    return jax.shard_map(
        local,
        mesh=grid,
        in_specs=(P(None, None, freq, tile), P(freq, tile, None), P(), P()),
        out_specs=(P(None, freq, tile, None), P(tile, freq)),
        check_vma=False,
    )
```

```python
import math

import jax
import jax.numpy as jnp
import numpy as np
from jax import lax
from jax.experimental import pallas as pl
from jax.experimental.pallas import tpu as pltpu
from jax.sharding import Mesh
from jax.sharding import PartitionSpec as P

depth_step = 0.5
omega_top = 2.8
slots = 128
size = 512
tile_size = 128
freq = ("y4", "y2", "y1", "w", "z4", "z2", "z1")
mixed = ("z1", "y1", "w", "z2", "y2", "z4", "y4")


def place_of(slot):
    bits = {axis: slot >> (len(freq) - 1 - at) & 1 for at, axis in enumerate(freq)}
    return sum(bits[axis] << (len(mixed) - 1 - at) for at, axis in enumerate(mixed))


def dft_table(length):
    places = np.arange(length)
    angles = 2.0 * np.pi / length * (places[:, None] * places[None, :] % length)
    both = np.concatenate([np.cos(angles), np.sin(angles)])
    return (both * (1.0 / math.sqrt(length))).astype(jnp.bfloat16)


def dot(left, right):
    return jnp.dot(left, right, preferred_element_type=jnp.float32)


def series(square, first, last):
    total = (-1.0) ** ((last - first) // 2) / math.factorial(last)
    for order in range(last - 2, first - 1, -2):
        total = (-1.0) ** ((order - first) // 2) / math.factorial(order) + square * total
    return total


def pick_kernel(owner_ref, rows_ref, out_ref):
    rows = rows_ref[owner_ref[0] // 2 % 16].astype(jnp.float32)
    for l in range(2):
        for c in range(2):
            lanes = (c * tile_size, (2 + c) * tile_size)
            piece = jnp.concatenate([rows[4 * l : 4 * l + 4, lane : lane + tile_size] for lane in lanes], axis=0)
            piece = piece.astype(jnp.bfloat16)
            for u in range(4):
                for h in range(2):
                    out_ref[((u * 2 + l) * 2 + h) * 2 + c] = piece


def shift_kernel(slot_ref, ids_ref, shift_ref):
    angular = omega_top * (ids_ref[slot_ref[0]] + 1).astype(jnp.float32) / slots

    def square(start, shape, axis):
        places = lax.broadcasted_iota(jnp.int32, shape, axis) + start
        signed = jnp.where(places < size // 2, places, places - size)
        return (2.0 * math.pi / size * signed.astype(jnp.float32)) ** 2

    ky_square = square(0, (16, size), 1)

    @pl.loop(0, size, step=16)
    def _(start):
        start = pl.multiple_of(start, 16)
        vertical = angular * angular - square(start, (16, size), 0) - ky_square
        root = depth_step * jnp.sqrt(jnp.abs(vertical))
        travel = jnp.where(vertical > 0.0, root, 0.0)
        damping = jnp.exp(jnp.where(vertical < 0.0, -root, 0.0))
        travel_square = travel * travel
        shift_ref[0, pl.ds(start, 16), :] = (damping * series(travel_square, 0, 12)).astype(jnp.bfloat16)
        shift_ref[1, pl.ds(start, 16), :] = (damping * travel * series(travel_square, 1, 13)).astype(jnp.bfloat16)


def pack_kernel(ids_ref, own_ref, other_ref, own_out, other_out, factor_ref):
    own_out[...] = own_ref[...]
    other_out[...] = other_ref[...]
    first = lax.broadcasted_iota(jnp.int32, (8, tile_size), 0) < 4
    for pair in range(slots // 2):
        low, high = (
            depth_step * (omega_top * (ids_ref[2 * pair + at] + 1).astype(jnp.float32) / slots) for at in range(2)
        )
        factor_ref[pair] = jnp.where(first, low, high)


def lens_kernel(place_ref, slow_ref, own_ref, other_ref, factor_ref, out_ref):
    slow = slow_ref[place_ref[0]].astype(jnp.float32) - 1.0
    halves = (jnp.concatenate([slow[:4]] * 2, axis=0), jnp.concatenate([slow[4:]] * 2, axis=0))
    low = place_ref[1] == 0
    depths = (jnp.where(low, halves[0], halves[1]), jnp.where(low, halves[1], halves[0]))
    for pair in range(slots // 2):
        factor = factor_ref[pair]
        for block, (ref, depth) in enumerate(zip((own_ref, other_ref), depths)):
            phase = factor * depth
            square = phase * phase
            lens_cos = series(square, 0, 8)
            lens_sin = phase * series(square, 1, 9)
            wave_real = ref[0, pair].astype(jnp.float32)
            wave_imag = ref[1, pair].astype(jnp.float32)
            real = wave_real * lens_cos - wave_imag * lens_sin
            imag = wave_real * lens_sin + wave_imag * lens_cos
            lanes = slice(block * tile_size, (block + 1) * tile_size)
            out_ref[place_of(2 * pair), :, lanes] = jnp.concatenate([real[:4], imag[:4]], axis=0).astype(jnp.bfloat16)
            out_ref[place_of(2 * pair + 1), :, lanes] = jnp.concatenate([real[4:], imag[4:]], axis=0).astype(jnp.bfloat16)


def column_kernel(table_ref, wave_ref, out_ref, both):
    for at in range(0, size // 4, 4):
        tiles = [wave_ref[place_of(at + k)].astype(jnp.float32) for k in range(4)]
        for part in range(2):
            rows = jnp.concatenate([tile[4 * part : 4 * part + 4] for tile in tiles], axis=0)
            both[4 * at : 4 * at + 16, part * 2 * tile_size : (part + 1) * 2 * tile_size] = rows.astype(jnp.bfloat16)
    by_cos = dot(table_ref[:size], both[...])
    by_sin = dot(table_ref[size:], both[...])
    real = (by_cos[:, : 2 * tile_size] + by_sin[:, 2 * tile_size :]).astype(jnp.bfloat16)
    imag = (by_cos[:, 2 * tile_size :] - by_sin[:, : 2 * tile_size]).astype(jnp.bfloat16)
    for block in range(2):
        lanes = slice(block * tile_size, (block + 1) * tile_size)
        out_ref[block, 0] = real[:, lanes]
        out_ref[block, 1] = imag[:, lanes]


def step_kernel(tile_ref, own_ref, other_ref, table_ref, shift_ref, wave_ref, image_ref, field, back):
    tile = tile_ref[0]
    for flip in range(4):
        block = (own_ref, other_ref)[flip % 2]
        start = pl.multiple_of((tile ^ flip) * tile_size, tile_size)
        real, imag = block[flip // 2, 0], block[flip // 2, 1]
        field[:size, pl.ds(start, tile_size)] = real
        field[size:, pl.ds(start, tile_size)] = imag
        start = pl.multiple_of(start + size, tile_size)
        field[:size, pl.ds(start, tile_size)] = imag
        field[size:, pl.ds(start, tile_size)] = -real
    start = pl.multiple_of(tile * tile_size, tile_size)
    cos_rows = table_ref[pl.ds(start, tile_size), :]
    sin_rows = table_ref[pl.ds(pl.multiple_of(start + size, tile_size), tile_size), :]
    inverse = jnp.concatenate(
        [jnp.concatenate([cos_rows, -sin_rows], axis=1), jnp.concatenate([sin_rows, cos_rows], axis=1)], axis=0
    )
    width = 256
    for at in range(0, size, width):
        part = slice(at, at + width)
        far = slice(at + size, at + size + width)
        spectrum = dot(field[...], table_ref[:, part])
        spec_real, spec_imag = spectrum[:size], spectrum[size:]
        shift_real = shift_ref[0, :, part].astype(jnp.float32)
        shift_imag = shift_ref[1, :, part].astype(jnp.float32)
        shifted_real = (spec_real * shift_real - spec_imag * shift_imag).astype(jnp.bfloat16)
        shifted_imag = (spec_real * shift_imag + spec_imag * shift_real).astype(jnp.bfloat16)
        rows = dot(inverse, jnp.concatenate([shifted_real, shifted_imag], axis=0)).astype(jnp.bfloat16)
        back[:, part] = rows
        back[:tile_size, far] = -rows[tile_size:]
        back[tile_size:, far] = rows[:tile_size]
    for at in range(0, size, width):
        part = slice(at, at + width)
        rows = dot(back[...], table_ref[:, part])
        wave_ref[0, :, part] = rows[:tile_size].astype(jnp.bfloat16)
        wave_ref[1, :, part] = rows[tile_size:].astype(jnp.bfloat16)
        image = (rows[:tile_size] * (1.0 / math.sqrt(slots))).T.astype(jnp.bfloat16)
        for slot in range(at // 4, (at + width) // 4):
            image_ref[place_of(slot)] = image[4 * slot - at : 4 * slot - at + 4]


def whole(memory=pltpu.VMEM):
    return pl.BlockSpec(memory_space=memory)


def exchange(x, axes):
    return lax.all_to_all(x, axes, split_axis=0, concat_axis=0, tiled=True)


def local(wavefield, slowness, freq_ids, depth_owner):
    owner = depth_owner[0]
    swap = [(0, 1), (1, 0)]
    side = lax.axis_index("h").astype(jnp.int32)
    tile = 2 * side + lax.axis_index("c").astype(jnp.int32)
    wavefield = wavefield.reshape(2, slots // 2, 8, tile_size)
    pieces = exchange(slowness.reshape(16, 8, size), ("y1", "w", "z4", "z2"))
    other = lax.ppermute(wavefield, "h", swap)
    pieces = pl.pallas_call(
        pick_kernel,
        out_shape=jax.ShapeDtypeStruct((32, 8, tile_size), jnp.bfloat16),
        in_specs=[whole(pltpu.SMEM), whole()],
        out_specs=whole(),
        compiler_params=pltpu.CompilerParams(vmem_limit_bytes=8 << 20),
        cost_estimate=pl.CostEstimate(flops=10_000, bytes_accessed=100_000, transcendentals=0),
    )(depth_owner, pieces)
    pieces = exchange(pieces, ("y4", "y2", "z1", "h", "c"))
    half = jax.ShapeDtypeStruct((2, slots // 2, 8, tile_size), jnp.bfloat16)
    own, other, factors = pl.pallas_call(
        pack_kernel,
        out_shape=(half, half, jax.ShapeDtypeStruct((slots // 2, 8, tile_size), jnp.float32)),
        in_specs=[whole(pltpu.SMEM)] + [whole()] * 2,
        out_specs=(whole(), whole(), whole()),
        compiler_params=pltpu.CompilerParams(vmem_limit_bytes=8 << 20),
        cost_estimate=pl.CostEstimate(flops=300_000, bytes_accessed=1_300_000, transcendentals=0),
    )(freq_ids, wavefield, other)
    place = (owner // 32 * 2 + owner % 2) * 4 + lax.axis_index(("y4", "y2")).astype(jnp.int32)
    lensed = pl.pallas_call(
        lens_kernel,
        out_shape=jax.ShapeDtypeStruct((slots, 8, 2 * tile_size), jnp.bfloat16),
        in_specs=[whole(pltpu.SMEM)] + [whole()] * 4,
        out_specs=whole(),
        compiler_params=pltpu.CompilerParams(vmem_limit_bytes=8 << 20),
        cost_estimate=pl.CostEstimate(flops=6_000_000, bytes_accessed=1_300_000, transcendentals=0),
    )(jnp.stack([place, side]), pieces, own, other, factors)
    columns = exchange(lensed, mixed)

    shift = pl.pallas_call(
        shift_kernel,
        out_shape=jax.ShapeDtypeStruct((2, size, size), jnp.bfloat16),
        in_specs=[whole(pltpu.SMEM)] * 2,
        out_specs=whole(),
        compiler_params=pltpu.CompilerParams(vmem_limit_bytes=16 << 20),
        cost_estimate=pl.CostEstimate(flops=10_000_000, bytes_accessed=2_100_000, transcendentals=500_000),
    )(lax.axis_index(freq).astype(jnp.int32)[None], freq_ids)
    columns, shift = lax.optimization_barrier((columns, shift))

    table = jnp.asarray(dft_table(size))
    own = pl.pallas_call(
        column_kernel,
        out_shape=jax.ShapeDtypeStruct((2, 2, size, tile_size), jnp.bfloat16),
        in_specs=[whole()] * 2,
        out_specs=whole(),
        scratch_shapes=[pltpu.VMEM((size, 4 * tile_size), jnp.bfloat16)],
        compiler_params=pltpu.CompilerParams(vmem_limit_bytes=8 << 20),
        cost_estimate=pl.CostEstimate(flops=540_000_000, bytes_accessed=2_100_000, transcendentals=0),
    )(table, columns)
    beside = lax.ppermute(own, "c", swap)
    wave_next, parts = pl.pallas_call(
        step_kernel,
        out_shape=(
            jax.ShapeDtypeStruct((2, tile_size, size), jnp.bfloat16),
            jax.ShapeDtypeStruct((slots, size // slots, tile_size), jnp.bfloat16),
        ),
        in_specs=[whole(pltpu.SMEM)] + [whole()] * 4,
        out_specs=(whole(), whole()),
        scratch_shapes=[
            pltpu.VMEM((2 * size, 2 * size), jnp.bfloat16),
            pltpu.VMEM((2 * tile_size, 2 * size), jnp.bfloat16),
        ],
        compiler_params=pltpu.CompilerParams(vmem_limit_bytes=20 << 20),
        cost_estimate=pl.CostEstimate(flops=1_620_000_000, bytes_accessed=4_600_000, transcendentals=0),
    )(tile[None], own, beside, table, shift)
    parts = exchange(parts, mixed)
    image = jnp.sum(parts.astype(jnp.float32), axis=0).T
    return (wave_next[:, None], image)


def solution(mesh):
    grid = Mesh(mesh.devices.reshape((2,) * 9), freq + ("h", "c"))
    tile = ("h", "c")
    return jax.shard_map(
        local,
        mesh=grid,
        in_specs=(P(None, None, freq, tile), P(freq, tile, None), P(), P()),
        out_specs=(P(None, freq, tile, None), P(tile, freq)),
        check_vma=False,
    )
```

```python
import math

import jax
import jax.numpy as jnp
import numpy as np
from jax import lax
from jax.experimental import pallas as pl
from jax.experimental.pallas import tpu as pltpu
from jax.sharding import Mesh
from jax.sharding import PartitionSpec as P

depth_step = 0.5
omega_top = 2.8
slots = 128
size = 512
tile_size = 128
freq = ("y4", "y2", "y1", "w", "z4", "z2", "z1")
mixed = ("z1", "y1", "w", "z2", "y2", "z4", "y4")


def place_of(slot):
    bits = {axis: slot >> (len(freq) - 1 - at) & 1 for at, axis in enumerate(freq)}
    return sum(bits[axis] << (len(mixed) - 1 - at) for at, axis in enumerate(mixed))


def dft_table(length):
    places = np.arange(length)
    angles = 2.0 * np.pi / length * (places[:, None] * places[None, :] % length)
    factor = 1.0 / math.sqrt(length)
    return (
        (np.cos(angles) * factor).astype(jnp.bfloat16),
        (np.sin(angles) * factor).astype(jnp.bfloat16),
    )


def dot(left, right):
    return jnp.dot(left, right, preferred_element_type=jnp.float32)


def series(square, first, last):
    total = (-1.0) ** ((last - first) // 2) / math.factorial(last)
    for order in range(last - 2, first - 1, -2):
        total = (-1.0) ** ((order - first) // 2) / math.factorial(order) + square * total
    return total


def rows_kernel(slow_ref, out_ref):
    for at in range(0, 32, 4):
        slow = slow_ref[0, 4 * at : 4 * at + 16, :].astype(jnp.float32)
        for k in range(4):
            out_ref[at + k] = slow[4 * k : 4 * k + 4].astype(jnp.bfloat16)


def pick_kernel(owner_ref, rows_ref, out_ref):
    rows = rows_ref[owner_ref[0] % 32].astype(jnp.float32)
    for c in range(2):
        lanes = (c * tile_size, (2 + c) * tile_size)
        piece = jnp.concatenate([rows[:, lane : lane + tile_size] for lane in lanes], axis=0).astype(jnp.bfloat16)
        for u in range(4):
            for h in range(2):
                out_ref[(u * 2 + h) * 2 + c] = piece


def shift_kernel(slot_ref, ids_ref, shift_ref):
    angular = omega_top * (ids_ref[slot_ref[0]] + 1).astype(jnp.float32) / slots

    def square(start, shape, axis):
        places = lax.broadcasted_iota(jnp.int32, shape, axis) + start
        signed = jnp.where(places < size // 2, places, places - size)
        return (2.0 * math.pi / size * signed.astype(jnp.float32)) ** 2

    ky_square = square(0, (16, size), 1)

    @pl.loop(0, size, step=16)
    def _(start):
        start = pl.multiple_of(start, 16)
        vertical = angular * angular - square(start, (16, size), 0) - ky_square
        root = depth_step * jnp.sqrt(jnp.abs(vertical))
        travel = jnp.where(vertical > 0.0, root, 0.0)
        damping = jnp.exp(jnp.where(vertical < 0.0, -root, 0.0))
        travel_square = travel * travel
        shift_ref[0, pl.ds(start, 16), :] = (damping * series(travel_square, 0, 12)).astype(jnp.bfloat16)
        shift_ref[1, pl.ds(start, 16), :] = (damping * travel * series(travel_square, 1, 13)).astype(jnp.bfloat16)


def pack_kernel(ids_ref, own_ref, other_ref, own_out, other_out, factor_ref):
    own_out[...] = own_ref[...]
    other_out[...] = other_ref[...]
    first = lax.broadcasted_iota(jnp.int32, (8, tile_size), 0) < 4
    for pair in range(slots // 2):
        low, high = (
            depth_step * (omega_top * (ids_ref[2 * pair + at] + 1).astype(jnp.float32) / slots) for at in range(2)
        )
        factor_ref[pair] = jnp.where(first, low, high)


def lens_kernel(place_ref, slow_ref, own_ref, other_ref, factor_ref, out_ref):
    slow = slow_ref[place_ref[0]].astype(jnp.float32) - 1.0
    halves = (jnp.concatenate([slow[:4]] * 2, axis=0), jnp.concatenate([slow[4:]] * 2, axis=0))
    low = place_ref[1] == 0
    depths = (jnp.where(low, halves[0], halves[1]), jnp.where(low, halves[1], halves[0]))
    for pair in range(slots // 2):
        factor = factor_ref[pair]
        for block, (ref, depth) in enumerate(zip((own_ref, other_ref), depths)):
            phase = factor * depth
            square = phase * phase
            lens_cos = series(square, 0, 8)
            lens_sin = phase * series(square, 1, 9)
            wave_real = ref[0, pair].astype(jnp.float32)
            wave_imag = ref[1, pair].astype(jnp.float32)
            real = wave_real * lens_cos - wave_imag * lens_sin
            imag = wave_real * lens_sin + wave_imag * lens_cos
            lanes = slice(block * tile_size, (block + 1) * tile_size)
            out_ref[place_of(2 * pair), :, lanes] = jnp.concatenate([real[:4], imag[:4]], axis=0).astype(jnp.bfloat16)
            out_ref[place_of(2 * pair + 1), :, lanes] = jnp.concatenate([real[4:], imag[4:]], axis=0).astype(jnp.bfloat16)


def column_kernel(cos_ref, sin_ref, wave_ref, out_ref, both):
    for at in range(0, size // 4, 4):
        tiles = [wave_ref[place_of(at + k)].astype(jnp.float32) for k in range(4)]
        for part in range(2):
            rows = jnp.concatenate([tile[4 * part : 4 * part + 4] for tile in tiles], axis=0)
            both[4 * at : 4 * at + 16, part * 2 * tile_size : (part + 1) * 2 * tile_size] = rows.astype(jnp.bfloat16)
    by_cos = dot(cos_ref[...], both[...])
    by_sin = dot(sin_ref[...], both[...])
    real = (by_cos[:, : 2 * tile_size] + by_sin[:, 2 * tile_size :]).astype(jnp.bfloat16)
    imag = (by_cos[:, 2 * tile_size :] - by_sin[:, : 2 * tile_size]).astype(jnp.bfloat16)
    for block in range(2):
        lanes = slice(block * tile_size, (block + 1) * tile_size)
        out_ref[block, 0] = real[:, lanes]
        out_ref[block, 1] = imag[:, lanes]


def step_kernel(tile_ref, own_ref, other_ref, cos_ref, sin_ref, shift_ref, wave_ref, image_ref, field, back):
    tile = tile_ref[0]
    for flip in range(4):
        block = (own_ref, other_ref)[flip % 2]
        start = pl.multiple_of((tile ^ flip) * tile_size, tile_size)
        field[:, :, pl.ds(start, tile_size)] = block[flip // 2]
    rows = pl.ds(pl.multiple_of(tile * tile_size, tile_size), tile_size)
    inverse = jnp.concatenate([cos_ref[rows, :], sin_ref[rows, :]], axis=0)
    width = 256
    for at in range(0, size, width):
        part = slice(at, at + width)
        spec_real = dot(field[0], cos_ref[:, part]) + dot(field[1], sin_ref[:, part])
        spec_imag = dot(field[1], cos_ref[:, part]) - dot(field[0], sin_ref[:, part])
        shift_real = shift_ref[0, :, part].astype(jnp.float32)
        shift_imag = shift_ref[1, :, part].astype(jnp.float32)
        shifted_real = (spec_real * shift_real - spec_imag * shift_imag).astype(jnp.bfloat16)
        shifted_imag = (spec_real * shift_imag + spec_imag * shift_real).astype(jnp.bfloat16)
        from_real = dot(inverse, shifted_real)
        from_imag = dot(inverse, shifted_imag)
        back[:tile_size, part] = (from_real[:tile_size] - from_imag[tile_size:]).astype(jnp.bfloat16)
        back[tile_size:, part] = (from_imag[:tile_size] + from_real[tile_size:]).astype(jnp.bfloat16)
    for at in range(0, size, width):
        part = slice(at, at + width)
        by_cos = dot(back[...], cos_ref[:, part])
        by_sin = dot(back[...], sin_ref[:, part])
        field_real = by_cos[:tile_size] - by_sin[tile_size:]
        wave_ref[0, :, part] = field_real.astype(jnp.bfloat16)
        wave_ref[1, :, part] = (by_cos[tile_size:] + by_sin[:tile_size]).astype(jnp.bfloat16)
        image = (field_real * (1.0 / math.sqrt(slots))).T.astype(jnp.bfloat16)
        for slot in range(at // 4, (at + width) // 4):
            image_ref[place_of(slot)] = image[4 * slot - at : 4 * slot - at + 4]


def whole(memory=pltpu.VMEM):
    return pl.BlockSpec(memory_space=memory)


def exchange(x, axes):
    return lax.all_to_all(x, axes, split_axis=0, concat_axis=0, tiled=True)


def local(wavefield, slowness, freq_ids, depth_owner):
    owner = depth_owner[0]
    swap = [(0, 1), (1, 0)]
    side = lax.axis_index("h").astype(jnp.int32)
    tile = 2 * side + lax.axis_index("c").astype(jnp.int32)
    wavefield = wavefield.reshape(2, slots // 2, 8, tile_size)
    pieces = pl.pallas_call(
        rows_kernel,
        out_shape=jax.ShapeDtypeStruct((32, 4, size), jnp.bfloat16),
        in_specs=[whole()],
        out_specs=whole(),
        compiler_params=pltpu.CompilerParams(vmem_limit_bytes=8 << 20),
        cost_estimate=pl.CostEstimate(flops=10_000, bytes_accessed=260_000, transcendentals=0),
    )(slowness)
    pieces = exchange(pieces, ("y1", "w", "z4", "z2", "z1"))
    other = lax.ppermute(wavefield, "h", swap)
    pieces = pl.pallas_call(
        pick_kernel,
        out_shape=jax.ShapeDtypeStruct((16, 8, tile_size), jnp.bfloat16),
        in_specs=[whole(pltpu.SMEM), whole()],
        out_specs=whole(),
        compiler_params=pltpu.CompilerParams(vmem_limit_bytes=8 << 20),
        cost_estimate=pl.CostEstimate(flops=10_000, bytes_accessed=100_000, transcendentals=0),
    )(depth_owner, pieces)
    pieces = exchange(pieces, ("y4", "y2", "h", "c"))
    half = jax.ShapeDtypeStruct((2, slots // 2, 8, tile_size), jnp.bfloat16)
    own, other, factors = pl.pallas_call(
        pack_kernel,
        out_shape=(half, half, jax.ShapeDtypeStruct((slots // 2, 8, tile_size), jnp.float32)),
        in_specs=[whole(pltpu.SMEM)] + [whole()] * 2,
        out_specs=(whole(), whole(), whole()),
        compiler_params=pltpu.CompilerParams(vmem_limit_bytes=8 << 20),
        cost_estimate=pl.CostEstimate(flops=300_000, bytes_accessed=1_300_000, transcendentals=0),
    )(freq_ids, wavefield, other)
    place = owner // 32 * 4 + lax.axis_index(("y4", "y2")).astype(jnp.int32)
    lensed = pl.pallas_call(
        lens_kernel,
        out_shape=jax.ShapeDtypeStruct((slots, 8, 2 * tile_size), jnp.bfloat16),
        in_specs=[whole(pltpu.SMEM)] + [whole()] * 4,
        out_specs=whole(),
        compiler_params=pltpu.CompilerParams(vmem_limit_bytes=8 << 20),
        cost_estimate=pl.CostEstimate(flops=6_000_000, bytes_accessed=1_300_000, transcendentals=0),
    )(jnp.stack([place, side]), pieces, own, other, factors)
    columns = exchange(lensed, mixed)

    table_cos, table_sin = dft_table(size)
    shift = pl.pallas_call(
        shift_kernel,
        out_shape=jax.ShapeDtypeStruct((2, size, size), jnp.bfloat16),
        in_specs=[whole(pltpu.SMEM)] * 2,
        out_specs=whole(),
        compiler_params=pltpu.CompilerParams(vmem_limit_bytes=16 << 20),
        cost_estimate=pl.CostEstimate(flops=10_000_000, bytes_accessed=2_100_000, transcendentals=500_000),
    )(lax.axis_index(freq).astype(jnp.int32)[None], freq_ids)
    columns, shift = lax.optimization_barrier((columns, shift))

    table_cos, table_sin = jnp.asarray(table_cos), jnp.asarray(table_sin)
    own = pl.pallas_call(
        column_kernel,
        out_shape=jax.ShapeDtypeStruct((2, 2, size, tile_size), jnp.bfloat16),
        in_specs=[whole()] * 3,
        out_specs=whole(),
        scratch_shapes=[pltpu.VMEM((size, 4 * tile_size), jnp.bfloat16)],
        compiler_params=pltpu.CompilerParams(vmem_limit_bytes=8 << 20),
        cost_estimate=pl.CostEstimate(flops=540_000_000, bytes_accessed=2_100_000, transcendentals=0),
    )(table_cos, table_sin, columns)
    beside = lax.ppermute(own, "c", swap)
    wave_next, parts = pl.pallas_call(
        step_kernel,
        out_shape=(
            jax.ShapeDtypeStruct((2, tile_size, size), jnp.bfloat16),
            jax.ShapeDtypeStruct((slots, size // slots, tile_size), jnp.bfloat16),
        ),
        in_specs=[whole(pltpu.SMEM)] + [whole()] * 5,
        out_specs=(whole(), whole()),
        scratch_shapes=[
            pltpu.VMEM((2, size, size), jnp.bfloat16),
            pltpu.VMEM((2 * tile_size, size), jnp.bfloat16),
        ],
        compiler_params=pltpu.CompilerParams(vmem_limit_bytes=20 << 20),
        cost_estimate=pl.CostEstimate(flops=1_620_000_000, bytes_accessed=4_600_000, transcendentals=0),
    )(tile[None], own, beside, table_cos, table_sin, shift)
    parts = exchange(parts, mixed)
    image = jnp.sum(parts.astype(jnp.float32), axis=0).T
    return (wave_next[:, None], image)


def solution(mesh):
    grid = Mesh(mesh.devices.reshape((2,) * 9), freq + ("h", "c"))
    tile = ("h", "c")
    return jax.shard_map(
        local,
        mesh=grid,
        in_specs=(P(None, None, freq, tile), P(freq, tile, None), P(), P()),
        out_specs=(P(None, freq, tile, None), P(tile, freq)),
        check_vma=False,
    )
```

```python
import math

import jax
import jax.numpy as jnp
import numpy as np
from jax import lax
from jax.experimental import pallas as pl
from jax.experimental.pallas import tpu as pltpu
from jax.sharding import Mesh
from jax.sharding import PartitionSpec as P

depth_step = 0.5
omega_top = 2.8
slots = 128
size = 512
tile_size = 128
freq = ("y4", "y2", "y1", "w", "z4", "z2", "z1")


def dft_table(length):
    places = np.arange(length)
    angles = 2.0 * np.pi / length * (places[:, None] * places[None, :] % length)
    factor = 1.0 / math.sqrt(length)
    return (
        (np.cos(angles) * factor).astype(jnp.bfloat16),
        (np.sin(angles) * factor).astype(jnp.bfloat16),
    )


def dot(left, right):
    return jnp.dot(left, right, preferred_element_type=jnp.float32)


def series(square, first, last):
    total = (-1.0) ** ((last - first) // 2) / math.factorial(last)
    for order in range(last - 2, first - 1, -2):
        total = (-1.0) ** ((order - first) // 2) / math.factorial(order) + square * total
    return total


def rows_kernel(slow_ref, out_ref):
    for at in range(0, 32, 4):
        slow = slow_ref[0, 4 * at : 4 * at + 16, :].astype(jnp.float32)
        for k in range(4):
            out_ref[at + k] = slow[4 * k : 4 * k + 4].astype(jnp.bfloat16)


def pick_kernel(owner_ref, rows_ref, out_ref):
    rows = rows_ref[owner_ref[0] % 32].astype(jnp.float32)
    for c in range(2):
        lanes = (c * tile_size, (2 + c) * tile_size)
        piece = jnp.concatenate([rows[:, lane : lane + tile_size] for lane in lanes], axis=0).astype(jnp.bfloat16)
        for u in range(4):
            for h in range(2):
                out_ref[(u * 2 + h) * 2 + c] = piece


def shift_kernel(slot_ref, ids_ref, shift_ref):
    angular = omega_top * (ids_ref[slot_ref[0]] + 1).astype(jnp.float32) / slots

    def square(start, shape, axis):
        places = lax.broadcasted_iota(jnp.int32, shape, axis) + start
        signed = jnp.where(places < size // 2, places, places - size)
        return (2.0 * math.pi / size * signed.astype(jnp.float32)) ** 2

    ky_square = square(0, (16, size), 1)

    @pl.loop(0, size, step=16)
    def _(start):
        start = pl.multiple_of(start, 16)
        vertical = angular * angular - square(start, (16, size), 0) - ky_square
        root = depth_step * jnp.sqrt(jnp.abs(vertical))
        travel = jnp.where(vertical > 0.0, root, 0.0)
        damping = jnp.exp(jnp.where(vertical < 0.0, -root, 0.0))
        travel_square = travel * travel
        shift_ref[0, pl.ds(start, 16), :] = (damping * series(travel_square, 0, 12)).astype(jnp.bfloat16)
        shift_ref[1, pl.ds(start, 16), :] = (damping * travel * series(travel_square, 1, 13)).astype(jnp.bfloat16)


def pack_kernel(ids_ref, own_ref, other_ref, own_out, other_out, factor_ref):
    own_out[...] = own_ref[...]
    other_out[...] = other_ref[...]
    first = lax.broadcasted_iota(jnp.int32, (8, tile_size), 0) < 4
    for pair in range(slots // 2):
        low, high = (
            depth_step * (omega_top * (ids_ref[2 * pair + at] + 1).astype(jnp.float32) / slots) for at in range(2)
        )
        factor_ref[pair] = jnp.where(first, low, high)


def lens_kernel(place_ref, slow_ref, own_ref, other_ref, factor_ref, out_ref, rows, sems):
    slow = slow_ref[place_ref[0]].astype(jnp.float32) - 1.0
    halves = (jnp.concatenate([slow[:4]] * 2, axis=0), jnp.concatenate([slow[4:]] * 2, axis=0))
    low = place_ref[1] == 0
    depths = (jnp.where(low, halves[0], halves[1]), jnp.where(low, halves[1], halves[0]))
    copies = []
    for quarter in range(4):
        for pair in range(quarter * slots // 8, (quarter + 1) * slots // 8):
            factor = factor_ref[pair]
            for block, (ref, depth) in enumerate(zip((own_ref, other_ref), depths)):
                phase = factor * depth
                square = phase * phase
                lens_cos = series(square, 0, 8)
                lens_sin = phase * series(square, 1, 9)
                wave_real = ref[0, pair].astype(jnp.float32)
                wave_imag = ref[1, pair].astype(jnp.float32)
                real = wave_real * lens_cos - wave_imag * lens_sin
                imag = wave_real * lens_sin + wave_imag * lens_cos
                both = jnp.concatenate([real[:4], imag[:4], real[4:], imag[4:]], axis=0).astype(jnp.bfloat16)
                rows[16 * pair : 16 * pair + 16, block * tile_size : (block + 1) * tile_size] = both
        part = pl.ds(quarter * 2 * slots, 2 * slots)
        copies.append(pltpu.make_async_copy(rows.at[part], out_ref.at[part], sems.at[quarter]))
        copies[-1].start()
    for copy in copies:
        copy.wait()


def column_kernel(cos_ref, sin_ref, wave_ref, out_ref, both):
    for at in range(0, size // 4, 4):
        tiles = [wave_ref[at + k].astype(jnp.float32) for k in range(4)]
        for part in range(2):
            rows = jnp.concatenate([tile[4 * part : 4 * part + 4] for tile in tiles], axis=0)
            both[4 * at : 4 * at + 16, part * 2 * tile_size : (part + 1) * 2 * tile_size] = rows.astype(jnp.bfloat16)
    by_cos = dot(cos_ref[...], both[...])
    by_sin = dot(sin_ref[...], both[...])
    real = (by_cos[:, : 2 * tile_size] + by_sin[:, 2 * tile_size :]).astype(jnp.bfloat16)
    imag = (by_cos[:, 2 * tile_size :] - by_sin[:, : 2 * tile_size]).astype(jnp.bfloat16)
    for block in range(2):
        lanes = slice(block * tile_size, (block + 1) * tile_size)
        out_ref[block, 0] = real[:, lanes]
        out_ref[block, 1] = imag[:, lanes]


def step_kernel(tile_ref, own_ref, other_ref, cos_ref, sin_ref, shift_ref, wave_ref, image_ref, field, back, waves, sem):
    tile = tile_ref[0]
    for flip in range(4):
        block = (own_ref, other_ref)[flip % 2]
        start = pl.multiple_of((tile ^ flip) * tile_size, tile_size)
        field[:, :, pl.ds(start, tile_size)] = block[flip // 2]
    rows = pl.ds(pl.multiple_of(tile * tile_size, tile_size), tile_size)
    inverse = jnp.concatenate([cos_ref[rows, :], sin_ref[rows, :]], axis=0)
    width = 256
    for at in range(0, size, width):
        part = slice(at, at + width)
        spec_real = dot(field[0], cos_ref[:, part]) + dot(field[1], sin_ref[:, part])
        spec_imag = dot(field[1], cos_ref[:, part]) - dot(field[0], sin_ref[:, part])
        shift_real = shift_ref[0, :, part].astype(jnp.float32)
        shift_imag = shift_ref[1, :, part].astype(jnp.float32)
        shifted_real = (spec_real * shift_real - spec_imag * shift_imag).astype(jnp.bfloat16)
        shifted_imag = (spec_real * shift_imag + spec_imag * shift_real).astype(jnp.bfloat16)
        from_real = dot(inverse, shifted_real)
        from_imag = dot(inverse, shifted_imag)
        back[:tile_size, part] = (from_real[:tile_size] - from_imag[tile_size:]).astype(jnp.bfloat16)
        back[tile_size:, part] = (from_imag[:tile_size] + from_real[tile_size:]).astype(jnp.bfloat16)
    reals = []
    for at in range(0, size, width):
        part = slice(at, at + width)
        by_cos = dot(back[...], cos_ref[:, part])
        by_sin = dot(back[...], sin_ref[:, part])
        reals.append(by_cos[:tile_size] - by_sin[tile_size:])
        waves[0, :, part] = reals[-1].astype(jnp.bfloat16)
        waves[1, :, part] = (by_cos[tile_size:] + by_sin[:tile_size]).astype(jnp.bfloat16)
    copy = pltpu.make_async_copy(waves, wave_ref, sem)
    copy.start()
    for at in range(0, size, width):
        image_ref[at : at + width, :] = (reals[at // width] * (1.0 / math.sqrt(slots))).T.astype(jnp.bfloat16)
    copy.wait()


def whole(memory=pltpu.VMEM):
    return pl.BlockSpec(memory_space=memory)


def exchange(x, axes):
    return lax.all_to_all(x, axes, split_axis=0, concat_axis=0, tiled=True)


def local(wavefield, slowness, freq_ids, depth_owner):
    owner = depth_owner[0]
    swap = [(0, 1), (1, 0)]
    side = lax.axis_index("h").astype(jnp.int32)
    tile = 2 * side + lax.axis_index("c").astype(jnp.int32)
    wavefield = wavefield.reshape(2, slots // 2, 8, tile_size)
    pieces = pl.pallas_call(
        rows_kernel,
        out_shape=jax.ShapeDtypeStruct((32, 4, size), jnp.bfloat16),
        in_specs=[whole()],
        out_specs=whole(),
        compiler_params=pltpu.CompilerParams(vmem_limit_bytes=8 << 20),
        cost_estimate=pl.CostEstimate(flops=10_000, bytes_accessed=260_000, transcendentals=0),
    )(slowness)
    pieces = exchange(pieces, ("y1", "w", "z4", "z2", "z1"))
    other = lax.ppermute(wavefield, "h", swap)
    pieces = pl.pallas_call(
        pick_kernel,
        out_shape=jax.ShapeDtypeStruct((16, 8, tile_size), jnp.bfloat16),
        in_specs=[whole(pltpu.SMEM), whole()],
        out_specs=whole(),
        compiler_params=pltpu.CompilerParams(vmem_limit_bytes=8 << 20),
        cost_estimate=pl.CostEstimate(flops=10_000, bytes_accessed=100_000, transcendentals=0),
    )(depth_owner, pieces)
    pieces = exchange(pieces, ("y4", "y2", "h", "c"))
    half = jax.ShapeDtypeStruct((2, slots // 2, 8, tile_size), jnp.bfloat16)
    own, other, factors = pl.pallas_call(
        pack_kernel,
        out_shape=(half, half, jax.ShapeDtypeStruct((slots // 2, 8, tile_size), jnp.float32)),
        in_specs=[whole(pltpu.SMEM)] + [whole()] * 2,
        out_specs=(whole(), whole(), whole()),
        compiler_params=pltpu.CompilerParams(vmem_limit_bytes=8 << 20),
        cost_estimate=pl.CostEstimate(flops=300_000, bytes_accessed=1_300_000, transcendentals=0),
    )(freq_ids, wavefield, other)
    place = owner // 32 * 4 + lax.axis_index(("y4", "y2")).astype(jnp.int32)
    lensed = pl.pallas_call(
        lens_kernel,
        out_shape=jax.ShapeDtypeStruct((8 * slots, 2 * tile_size), jnp.bfloat16),
        in_specs=[whole(pltpu.SMEM)] + [whole()] * 4,
        out_specs=whole(pl.ANY),
        scratch_shapes=[pltpu.VMEM((8 * slots, 2 * tile_size), jnp.bfloat16), pltpu.SemaphoreType.DMA((4,))],
        compiler_params=pltpu.CompilerParams(vmem_limit_bytes=8 << 20),
        cost_estimate=pl.CostEstimate(flops=6_000_000, bytes_accessed=1_300_000, transcendentals=0),
    )(jnp.stack([place, side]), pieces, own, other, factors)
    columns = exchange(lensed.reshape(slots, 8, 2 * tile_size), freq)

    table_cos, table_sin = dft_table(size)
    shift = pl.pallas_call(
        shift_kernel,
        out_shape=jax.ShapeDtypeStruct((2, size, size), jnp.bfloat16),
        in_specs=[whole(pltpu.SMEM)] * 2,
        out_specs=whole(),
        compiler_params=pltpu.CompilerParams(vmem_limit_bytes=16 << 20),
        cost_estimate=pl.CostEstimate(flops=10_000_000, bytes_accessed=2_100_000, transcendentals=500_000),
    )(lax.axis_index(freq).astype(jnp.int32)[None], freq_ids)
    columns, shift = lax.optimization_barrier((columns, shift))

    table_cos, table_sin = jnp.asarray(table_cos), jnp.asarray(table_sin)
    own = pl.pallas_call(
        column_kernel,
        out_shape=jax.ShapeDtypeStruct((2, 2, size, tile_size), jnp.bfloat16),
        in_specs=[whole()] * 3,
        out_specs=whole(),
        scratch_shapes=[pltpu.VMEM((size, 4 * tile_size), jnp.bfloat16)],
        compiler_params=pltpu.CompilerParams(vmem_limit_bytes=8 << 20),
        cost_estimate=pl.CostEstimate(flops=540_000_000, bytes_accessed=2_100_000, transcendentals=0),
    )(table_cos, table_sin, columns)
    beside = lax.ppermute(own, "c", swap)
    wave_next, parts = pl.pallas_call(
        step_kernel,
        out_shape=(
            jax.ShapeDtypeStruct((2, tile_size, size), jnp.bfloat16),
            jax.ShapeDtypeStruct((size, tile_size), jnp.bfloat16),
        ),
        in_specs=[whole(pltpu.SMEM)] + [whole()] * 5,
        out_specs=(whole(pl.ANY), whole()),
        scratch_shapes=[
            pltpu.VMEM((2, size, size), jnp.bfloat16),
            pltpu.VMEM((2 * tile_size, size), jnp.bfloat16),
            pltpu.VMEM((2, tile_size, size), jnp.bfloat16),
            pltpu.SemaphoreType.DMA,
        ],
        compiler_params=pltpu.CompilerParams(vmem_limit_bytes=20 << 20),
        cost_estimate=pl.CostEstimate(flops=1_620_000_000, bytes_accessed=4_600_000, transcendentals=0),
    )(tile[None], own, beside, table_cos, table_sin, shift)
    parts = exchange(parts.reshape(slots, size // slots, tile_size), freq)
    image = jnp.sum(parts.astype(jnp.float32), axis=0).T
    return (wave_next[:, None], image)


def solution(mesh):
    grid = Mesh(mesh.devices.reshape((2,) * 9), freq + ("h", "c"))
    tile = ("h", "c")
    return jax.shard_map(
        local,
        mesh=grid,
        in_specs=(P(None, None, freq, tile), P(freq, tile, None), P(), P()),
        out_specs=(P(None, freq, tile, None), P(tile, freq)),
        check_vma=False,
    )
```

```python
import math

import jax
import jax.numpy as jnp
import numpy as np
from jax import lax
from jax.experimental import pallas as pl
from jax.experimental.pallas import tpu as pltpu
from jax.sharding import Mesh
from jax.sharding import PartitionSpec as P

depth_step = 0.5
omega_top = 2.8
slots = 128
size = 512
tile_size = 128
freq = ("y4", "y2", "y1", "w", "z4", "z2", "z1")
mixed = ("z1", "y1", "w", "z2", "y2", "z4", "y4")


def place_of(slot):
    bits = {axis: slot >> (len(freq) - 1 - at) & 1 for at, axis in enumerate(freq)}
    return sum(bits[axis] << (len(mixed) - 1 - at) for at, axis in enumerate(mixed))


def dft_table(length):
    places = np.arange(length)
    angles = 2.0 * np.pi / length * (places[:, None] * places[None, :] % length)
    factor = 1.0 / math.sqrt(length)
    return (
        (np.cos(angles) * factor).astype(jnp.bfloat16),
        (np.sin(angles) * factor).astype(jnp.bfloat16),
    )


def dot(left, right):
    return jnp.dot(left, right, preferred_element_type=jnp.float32)


def series(square, first, last):
    total = (-1.0) ** ((last - first) // 2) / math.factorial(last)
    for order in range(last - 2, first - 1, -2):
        total = (-1.0) ** ((order - first) // 2) / math.factorial(order) + square * total
    return total


def rows_kernel(slow_ref, out_ref):
    for at in range(0, 32, 4):
        slow = slow_ref[0, 4 * at : 4 * at + 16, :].astype(jnp.float32)
        for k in range(4):
            out_ref[at + k] = slow[4 * k : 4 * k + 4].astype(jnp.bfloat16)


def pick_kernel(owner_ref, rows_ref, out_ref):
    rows = rows_ref[owner_ref[0] % 32].astype(jnp.float32)
    for c in range(2):
        lanes = (c * tile_size, (2 + c) * tile_size)
        piece = jnp.concatenate([rows[:, lane : lane + tile_size] for lane in lanes], axis=0).astype(jnp.bfloat16)
        for u in range(4):
            for h in range(2):
                out_ref[(u * 2 + h) * 2 + c] = piece


def shift_kernel(slot_ref, ids_ref, shift_ref):
    angular = omega_top * (ids_ref[slot_ref[0]] + 1).astype(jnp.float32) / slots

    def square(start, shape, axis):
        places = lax.broadcasted_iota(jnp.int32, shape, axis) + start
        signed = jnp.where(places < size // 2, places, places - size)
        return (2.0 * math.pi / size * signed.astype(jnp.float32)) ** 2

    ky_square = square(0, (16, size), 1)

    @pl.loop(0, size, step=16)
    def _(start):
        start = pl.multiple_of(start, 16)
        vertical = angular * angular - square(start, (16, size), 0) - ky_square
        root = depth_step * jnp.sqrt(jnp.abs(vertical))
        travel = jnp.where(vertical > 0.0, root, 0.0)
        damping = jnp.exp(jnp.where(vertical < 0.0, -root, 0.0))
        travel_square = travel * travel
        shift_ref[0, pl.ds(start, 16), :] = (damping * series(travel_square, 0, 12)).astype(jnp.bfloat16)
        shift_ref[1, pl.ds(start, 16), :] = (damping * travel * series(travel_square, 1, 13)).astype(jnp.bfloat16)


def pack_kernel(ids_ref, own_ref, other_ref, own_out, other_out, factor_ref):
    own_out[...] = own_ref[...]
    other_out[...] = other_ref[...]
    first = lax.broadcasted_iota(jnp.int32, (8, tile_size), 0) < 4
    for pair in range(slots // 2):
        low, high = (
            depth_step * (omega_top * (ids_ref[2 * pair + at] + 1).astype(jnp.float32) / slots) for at in range(2)
        )
        factor_ref[pair] = jnp.where(first, low, high)


def lens_kernel(place_ref, slow_ref, own_ref, other_ref, factor_ref, out_ref):
    slow = slow_ref[place_ref[0]].astype(jnp.float32) - 1.0
    halves = (jnp.concatenate([slow[:4]] * 2, axis=0), jnp.concatenate([slow[4:]] * 2, axis=0))
    low = place_ref[1] == 0
    depths = (jnp.where(low, halves[0], halves[1]), jnp.where(low, halves[1], halves[0]))
    for pair in range(slots // 2):
        factor = factor_ref[pair]
        for block, (ref, depth) in enumerate(zip((own_ref, other_ref), depths)):
            phase = factor * depth
            square = phase * phase
            lens_cos = series(square, 0, 8)
            lens_sin = phase * series(square, 1, 9)
            wave_real = ref[0, pair].astype(jnp.float32)
            wave_imag = ref[1, pair].astype(jnp.float32)
            real = wave_real * lens_cos - wave_imag * lens_sin
            imag = wave_real * lens_sin + wave_imag * lens_cos
            lanes = slice(block * tile_size, (block + 1) * tile_size)
            out_ref[place_of(2 * pair), :, lanes] = jnp.concatenate([real[:4], imag[:4]], axis=0).astype(jnp.bfloat16)
            out_ref[place_of(2 * pair + 1), :, lanes] = jnp.concatenate([real[4:], imag[4:]], axis=0).astype(jnp.bfloat16)


def column_kernel(cos_ref, sin_ref, wave_ref, out_ref, both):
    for at in range(0, size // 4, 4):
        tiles = [wave_ref[place_of(at + k)].astype(jnp.float32) for k in range(4)]
        for part in range(2):
            rows = jnp.concatenate([tile[4 * part : 4 * part + 4] for tile in tiles], axis=0)
            both[4 * at : 4 * at + 16, part * 2 * tile_size : (part + 1) * 2 * tile_size] = rows.astype(jnp.bfloat16)
    by_cos = dot(cos_ref[...], both[...])
    by_sin = dot(sin_ref[...], both[...])
    real = (by_cos[:, : 2 * tile_size] + by_sin[:, 2 * tile_size :]).astype(jnp.bfloat16)
    imag = (by_cos[:, 2 * tile_size :] - by_sin[:, : 2 * tile_size]).astype(jnp.bfloat16)
    for block in range(2):
        lanes = slice(block * tile_size, (block + 1) * tile_size)
        out_ref[block, 0] = real[:, lanes]
        out_ref[block, 1] = imag[:, lanes]


def half_transform(tile, flips, block_ref, cos_ref, sin_ref, field, use):
    starts = [pl.multiple_of((tile ^ flip) * tile_size, tile_size) for flip in flips]
    for at in range(2):
        field[:, :, at * tile_size : (at + 1) * tile_size] = block_ref[at]
    cos_rows, sin_rows = (
        jnp.concatenate([ref[pl.ds(start, tile_size), :] for start in starts], axis=0) for ref in (cos_ref, sin_ref)
    )
    width = 256
    for at in range(0, size, width):
        part = slice(at, at + width)
        real = dot(field[0], cos_rows[:, part]) + dot(field[1], sin_rows[:, part])
        imag = dot(field[1], cos_rows[:, part]) - dot(field[0], sin_rows[:, part])
        use(part, real, imag)


def near_kernel(tile_ref, own_ref, cos_ref, sin_ref, out_ref, field):
    def use(part, real, imag):
        out_ref[0, :, part] = real
        out_ref[1, :, part] = imag

    half_transform(tile_ref[0], (0, 2), own_ref, cos_ref, sin_ref, field, use)


def step_kernel(tile_ref, near_ref, other_ref, cos_ref, sin_ref, shift_ref, wave_ref, image_ref, field, back):
    tile = tile_ref[0]
    rows = pl.ds(pl.multiple_of(tile * tile_size, tile_size), tile_size)
    inverse = jnp.concatenate([cos_ref[rows, :], sin_ref[rows, :]], axis=0)
    width = 256

    def use(part, real, imag):
        spec_real = real + near_ref[0, :, part]
        spec_imag = imag + near_ref[1, :, part]
        shift_real = shift_ref[0, :, part].astype(jnp.float32)
        shift_imag = shift_ref[1, :, part].astype(jnp.float32)
        shifted_real = (spec_real * shift_real - spec_imag * shift_imag).astype(jnp.bfloat16)
        shifted_imag = (spec_real * shift_imag + spec_imag * shift_real).astype(jnp.bfloat16)
        from_real = dot(inverse, shifted_real)
        from_imag = dot(inverse, shifted_imag)
        back[:tile_size, part] = (from_real[:tile_size] - from_imag[tile_size:]).astype(jnp.bfloat16)
        back[tile_size:, part] = (from_imag[:tile_size] + from_real[tile_size:]).astype(jnp.bfloat16)

    half_transform(tile, (1, 3), other_ref, cos_ref, sin_ref, field, use)
    for at in range(0, size, width):
        part = slice(at, at + width)
        by_cos = dot(back[...], cos_ref[:, part])
        by_sin = dot(back[...], sin_ref[:, part])
        field_real = by_cos[:tile_size] - by_sin[tile_size:]
        wave_ref[0, :, part] = field_real.astype(jnp.bfloat16)
        wave_ref[1, :, part] = (by_cos[tile_size:] + by_sin[:tile_size]).astype(jnp.bfloat16)
        image = (field_real * (1.0 / math.sqrt(slots))).T.astype(jnp.bfloat16)
        for slot in range(at // 4, (at + width) // 4):
            image_ref[place_of(slot)] = image[4 * slot - at : 4 * slot - at + 4]


def whole(memory=pltpu.VMEM):
    return pl.BlockSpec(memory_space=memory)


def exchange(x, axes):
    return lax.all_to_all(x, axes, split_axis=0, concat_axis=0, tiled=True)


def local(wavefield, slowness, freq_ids, depth_owner):
    owner = depth_owner[0]
    swap = [(0, 1), (1, 0)]
    side = lax.axis_index("h").astype(jnp.int32)
    tile = 2 * side + lax.axis_index("c").astype(jnp.int32)
    wavefield = wavefield.reshape(2, slots // 2, 8, tile_size)
    pieces = pl.pallas_call(
        rows_kernel,
        out_shape=jax.ShapeDtypeStruct((32, 4, size), jnp.bfloat16),
        in_specs=[whole()],
        out_specs=whole(),
        compiler_params=pltpu.CompilerParams(vmem_limit_bytes=8 << 20),
        cost_estimate=pl.CostEstimate(flops=10_000, bytes_accessed=260_000, transcendentals=0),
    )(slowness)
    pieces = exchange(pieces, ("y1", "w", "z4", "z2", "z1"))
    other = lax.ppermute(wavefield, "h", swap)
    pieces = pl.pallas_call(
        pick_kernel,
        out_shape=jax.ShapeDtypeStruct((16, 8, tile_size), jnp.bfloat16),
        in_specs=[whole(pltpu.SMEM), whole()],
        out_specs=whole(),
        compiler_params=pltpu.CompilerParams(vmem_limit_bytes=8 << 20),
        cost_estimate=pl.CostEstimate(flops=10_000, bytes_accessed=100_000, transcendentals=0),
    )(depth_owner, pieces)
    pieces = exchange(pieces, ("y4", "y2", "h", "c"))
    half = jax.ShapeDtypeStruct((2, slots // 2, 8, tile_size), jnp.bfloat16)
    own, other, factors = pl.pallas_call(
        pack_kernel,
        out_shape=(half, half, jax.ShapeDtypeStruct((slots // 2, 8, tile_size), jnp.float32)),
        in_specs=[whole(pltpu.SMEM)] + [whole()] * 2,
        out_specs=(whole(), whole(), whole()),
        compiler_params=pltpu.CompilerParams(vmem_limit_bytes=8 << 20),
        cost_estimate=pl.CostEstimate(flops=300_000, bytes_accessed=1_300_000, transcendentals=0),
    )(freq_ids, wavefield, other)
    place = owner // 32 * 4 + lax.axis_index(("y4", "y2")).astype(jnp.int32)
    lensed = pl.pallas_call(
        lens_kernel,
        out_shape=jax.ShapeDtypeStruct((slots, 8, 2 * tile_size), jnp.bfloat16),
        in_specs=[whole(pltpu.SMEM)] + [whole()] * 4,
        out_specs=whole(),
        compiler_params=pltpu.CompilerParams(vmem_limit_bytes=8 << 20),
        cost_estimate=pl.CostEstimate(flops=6_000_000, bytes_accessed=1_300_000, transcendentals=0),
    )(jnp.stack([place, side]), pieces, own, other, factors)
    columns = exchange(lensed, mixed)

    table_cos, table_sin = dft_table(size)
    shift = pl.pallas_call(
        shift_kernel,
        out_shape=jax.ShapeDtypeStruct((2, size, size), jnp.bfloat16),
        in_specs=[whole(pltpu.SMEM)] * 2,
        out_specs=whole(),
        compiler_params=pltpu.CompilerParams(vmem_limit_bytes=16 << 20),
        cost_estimate=pl.CostEstimate(flops=10_000_000, bytes_accessed=2_100_000, transcendentals=500_000),
    )(lax.axis_index(freq).astype(jnp.int32)[None], freq_ids)
    columns, shift = lax.optimization_barrier((columns, shift))

    table_cos, table_sin = jnp.asarray(table_cos), jnp.asarray(table_sin)
    own = pl.pallas_call(
        column_kernel,
        out_shape=jax.ShapeDtypeStruct((2, 2, size, tile_size), jnp.bfloat16),
        in_specs=[whole()] * 3,
        out_specs=whole(),
        scratch_shapes=[pltpu.VMEM((size, 4 * tile_size), jnp.bfloat16)],
        compiler_params=pltpu.CompilerParams(vmem_limit_bytes=8 << 20),
        cost_estimate=pl.CostEstimate(flops=540_000_000, bytes_accessed=2_100_000, transcendentals=0),
    )(table_cos, table_sin, columns)
    beside = lax.ppermute(own, "c", swap)
    near = pl.pallas_call(
        near_kernel,
        out_shape=jax.ShapeDtypeStruct((2, size, size), jnp.float32),
        in_specs=[whole(pltpu.SMEM)] + [whole()] * 3,
        out_specs=whole(),
        scratch_shapes=[pltpu.VMEM((2, size, 2 * tile_size), jnp.bfloat16)],
        compiler_params=pltpu.CompilerParams(vmem_limit_bytes=12 << 20),
        cost_estimate=pl.CostEstimate(flops=540_000_000, bytes_accessed=3_600_000, transcendentals=0),
    )(tile[None], own, table_cos, table_sin)
    wave_next, parts = pl.pallas_call(
        step_kernel,
        out_shape=(
            jax.ShapeDtypeStruct((2, tile_size, size), jnp.bfloat16),
            jax.ShapeDtypeStruct((slots, size // slots, tile_size), jnp.bfloat16),
        ),
        in_specs=[whole(pltpu.SMEM)] + [whole()] * 5,
        out_specs=(whole(), whole()),
        scratch_shapes=[
            pltpu.VMEM((2, size, 2 * tile_size), jnp.bfloat16),
            pltpu.VMEM((2 * tile_size, size), jnp.bfloat16),
        ],
        compiler_params=pltpu.CompilerParams(vmem_limit_bytes=20 << 20),
        cost_estimate=pl.CostEstimate(flops=1_080_000_000, bytes_accessed=5_600_000, transcendentals=0),
    )(tile[None], near, beside, table_cos, table_sin, shift)
    parts = exchange(parts, mixed)
    image = jnp.sum(parts.astype(jnp.float32), axis=0).T
    return (wave_next[:, None], image)


def solution(mesh):
    grid = Mesh(mesh.devices.reshape((2,) * 9), freq + ("h", "c"))
    tile = ("h", "c")
    return jax.shard_map(
        local,
        mesh=grid,
        in_specs=(P(None, None, freq, tile), P(freq, tile, None), P(), P()),
        out_specs=(P(None, freq, tile, None), P(tile, freq)),
        check_vma=False,
    )
```

```python
import math

import jax
import jax.numpy as jnp
import numpy as np
from jax import lax
from jax.experimental import pallas as pl
from jax.experimental.pallas import tpu as pltpu
from jax.sharding import Mesh
from jax.sharding import PartitionSpec as P

depth_step = 0.5
omega_top = 2.8
slots = 128
size = 512
tile_size = 128
freq = ("y4", "y2", "y1", "w", "z4", "z2", "z1")


def dft_table(length):
    places = np.arange(length)
    angles = 2.0 * np.pi / length * (places[:, None] * places[None, :] % length)
    factor = 1.0 / math.sqrt(length)
    return (
        (np.cos(angles) * factor).astype(jnp.bfloat16),
        (np.sin(angles) * factor).astype(jnp.bfloat16),
    )


def dot(left, right):
    return jnp.dot(left, right, preferred_element_type=jnp.float32)


def series(square, first, last):
    total = (-1.0) ** ((last - first) // 2) / math.factorial(last)
    for order in range(last - 2, first - 1, -2):
        total = (-1.0) ** ((order - first) // 2) / math.factorial(order) + square * total
    return total


def rows_kernel(slow_ref, out_ref):
    for at in range(0, 32, 4):
        slow = slow_ref[0, 4 * at : 4 * at + 16, :].astype(jnp.float32)
        for k in range(4):
            out_ref[at + k] = slow[4 * k : 4 * k + 4].astype(jnp.bfloat16)


def pick_kernel(owner_ref, rows_ref, out_ref):
    rows = rows_ref[owner_ref[0] % 32].astype(jnp.float32)
    for c in range(2):
        lanes = (c * tile_size, (2 + c) * tile_size)
        piece = jnp.concatenate([rows[:, lane : lane + tile_size] for lane in lanes], axis=0).astype(jnp.bfloat16)
        for u in range(4):
            for h in range(2):
                out_ref[(u * 2 + h) * 2 + c] = piece


def shift_kernel(slot_ref, ids_ref, shift_ref):
    angular = omega_top * (ids_ref[slot_ref[0]] + 1).astype(jnp.float32) / slots

    def square(start, shape, axis):
        places = lax.broadcasted_iota(jnp.int32, shape, axis) + start
        signed = jnp.where(places < size // 2, places, places - size)
        return (2.0 * math.pi / size * signed.astype(jnp.float32)) ** 2

    ky_square = square(0, (16, size), 1)

    @pl.loop(0, size, step=16)
    def _(start):
        start = pl.multiple_of(start, 16)
        vertical = angular * angular - square(start, (16, size), 0) - ky_square
        root = depth_step * jnp.sqrt(jnp.abs(vertical))
        travel = jnp.where(vertical > 0.0, root, 0.0)
        damping = jnp.exp(jnp.where(vertical < 0.0, -root, 0.0))
        travel_square = travel * travel
        shift_ref[0, pl.ds(start, 16), :] = (damping * series(travel_square, 0, 12)).astype(jnp.bfloat16)
        shift_ref[1, pl.ds(start, 16), :] = (damping * travel * series(travel_square, 1, 13)).astype(jnp.bfloat16)


def pack_kernel(ids_ref, own_ref, other_ref, own_out, other_out, factor_ref):
    own_out[...] = own_ref[...]
    other_out[...] = other_ref[...]
    first = lax.broadcasted_iota(jnp.int32, (8, tile_size), 0) < 4
    for pair in range(slots // 2):
        low, high = (
            depth_step * (omega_top * (ids_ref[2 * pair + at] + 1).astype(jnp.float32) / slots) for at in range(2)
        )
        factor_ref[pair] = jnp.where(first, low, high)


def lens_kernel(place_ref, slow_ref, own_ref, other_ref, factor_ref, out_ref, rows, sems):
    slow = slow_ref[place_ref[0]].astype(jnp.float32) - 1.0
    halves = (jnp.concatenate([slow[:4]] * 2, axis=0), jnp.concatenate([slow[4:]] * 2, axis=0))
    low = place_ref[1] == 0
    depths = (jnp.where(low, halves[0], halves[1]), jnp.where(low, halves[1], halves[0]))
    copies = []
    for quarter in range(4):
        for pair in range(quarter * slots // 8, (quarter + 1) * slots // 8):
            factor = factor_ref[pair]
            for block, (ref, depth) in enumerate(zip((own_ref, other_ref), depths)):
                phase = factor * depth
                square = phase * phase
                lens_cos = series(square, 0, 8)
                lens_sin = phase * series(square, 1, 9)
                wave_real = ref[0, pair].astype(jnp.float32)
                wave_imag = ref[1, pair].astype(jnp.float32)
                real = wave_real * lens_cos - wave_imag * lens_sin
                imag = wave_real * lens_sin + wave_imag * lens_cos
                both = jnp.concatenate([real[:4], imag[:4], real[4:], imag[4:]], axis=0).astype(jnp.bfloat16)
                rows[16 * pair : 16 * pair + 16, block * tile_size : (block + 1) * tile_size] = both
        part = pl.ds(quarter * 2 * slots, 2 * slots)
        copies.append(pltpu.make_async_copy(rows.at[part], out_ref.at[part], sems.at[quarter]))
        copies[-1].start()
    for copy in copies:
        copy.wait()


def column_kernel(cos_ref, sin_ref, wave_ref, out_ref, both):
    for at in range(0, size // 4, 4):
        tiles = [wave_ref[at + k].astype(jnp.float32) for k in range(4)]
        for part in range(2):
            rows = jnp.concatenate([tile[4 * part : 4 * part + 4] for tile in tiles], axis=0)
            both[4 * at : 4 * at + 16, part * 2 * tile_size : (part + 1) * 2 * tile_size] = rows.astype(jnp.bfloat16)
    by_cos = dot(cos_ref[...], both[...])
    by_sin = dot(sin_ref[...], both[...])
    real = (by_cos[:, : 2 * tile_size] + by_sin[:, 2 * tile_size :]).astype(jnp.bfloat16)
    imag = (by_cos[:, 2 * tile_size :] - by_sin[:, : 2 * tile_size]).astype(jnp.bfloat16)
    for block in range(2):
        lanes = slice(block * tile_size, (block + 1) * tile_size)
        out_ref[block, 0] = real[:, lanes]
        out_ref[block, 1] = imag[:, lanes]


def half_transform(tile, flips, block_ref, cos_ref, sin_ref, field, use):
    starts = [pl.multiple_of((tile ^ flip) * tile_size, tile_size) for flip in flips]
    for at in range(2):
        field[:, :, at * tile_size : (at + 1) * tile_size] = block_ref[at]
    cos_rows, sin_rows = (
        jnp.concatenate([ref[pl.ds(start, tile_size), :] for start in starts], axis=0) for ref in (cos_ref, sin_ref)
    )
    width = 256
    for at in range(0, size, width):
        part = slice(at, at + width)
        real = dot(field[0], cos_rows[:, part]) + dot(field[1], sin_rows[:, part])
        imag = dot(field[1], cos_rows[:, part]) - dot(field[0], sin_rows[:, part])
        use(part, real, imag)


def near_kernel(tile_ref, own_ref, cos_ref, sin_ref, out_ref, field):
    def use(part, real, imag):
        out_ref[0, :, part] = real
        out_ref[1, :, part] = imag

    half_transform(tile_ref[0], (0, 2), own_ref, cos_ref, sin_ref, field, use)


def step_kernel(tile_ref, near_ref, other_ref, cos_ref, sin_ref, shift_ref, wave_ref, image_ref, field, back, waves, sem):
    tile = tile_ref[0]
    rows = pl.ds(pl.multiple_of(tile * tile_size, tile_size), tile_size)
    inverse = jnp.concatenate([cos_ref[rows, :], sin_ref[rows, :]], axis=0)
    width = 256

    def use(part, real, imag):
        spec_real = real + near_ref[0, :, part]
        spec_imag = imag + near_ref[1, :, part]
        shift_real = shift_ref[0, :, part].astype(jnp.float32)
        shift_imag = shift_ref[1, :, part].astype(jnp.float32)
        shifted_real = (spec_real * shift_real - spec_imag * shift_imag).astype(jnp.bfloat16)
        shifted_imag = (spec_real * shift_imag + spec_imag * shift_real).astype(jnp.bfloat16)
        from_real = dot(inverse, shifted_real)
        from_imag = dot(inverse, shifted_imag)
        back[:tile_size, part] = (from_real[:tile_size] - from_imag[tile_size:]).astype(jnp.bfloat16)
        back[tile_size:, part] = (from_imag[:tile_size] + from_real[tile_size:]).astype(jnp.bfloat16)

    half_transform(tile, (1, 3), other_ref, cos_ref, sin_ref, field, use)
    reals = []
    for at in range(0, size, width):
        part = slice(at, at + width)
        by_cos = dot(back[...], cos_ref[:, part])
        by_sin = dot(back[...], sin_ref[:, part])
        reals.append(by_cos[:tile_size] - by_sin[tile_size:])
        waves[0, :, part] = reals[-1].astype(jnp.bfloat16)
        waves[1, :, part] = (by_cos[tile_size:] + by_sin[:tile_size]).astype(jnp.bfloat16)
    copy = pltpu.make_async_copy(waves, wave_ref, sem)
    copy.start()
    for at in range(0, size, width):
        image_ref[at : at + width, :] = (reals[at // width] * (1.0 / math.sqrt(slots))).T.astype(jnp.bfloat16)
    copy.wait()


def whole(memory=pltpu.VMEM):
    return pl.BlockSpec(memory_space=memory)


def exchange(x, axes):
    return lax.all_to_all(x, axes, split_axis=0, concat_axis=0, tiled=True)


def local(wavefield, slowness, freq_ids, depth_owner):
    owner = depth_owner[0]
    swap = [(0, 1), (1, 0)]
    side = lax.axis_index("h").astype(jnp.int32)
    tile = 2 * side + lax.axis_index("c").astype(jnp.int32)
    wavefield = wavefield.reshape(2, slots // 2, 8, tile_size)
    pieces = pl.pallas_call(
        rows_kernel,
        out_shape=jax.ShapeDtypeStruct((32, 4, size), jnp.bfloat16),
        in_specs=[whole()],
        out_specs=whole(),
        compiler_params=pltpu.CompilerParams(vmem_limit_bytes=8 << 20),
        cost_estimate=pl.CostEstimate(flops=10_000, bytes_accessed=260_000, transcendentals=0),
    )(slowness)
    pieces = exchange(pieces, ("y1", "w", "z4", "z2", "z1"))
    other = lax.ppermute(wavefield, "h", swap)
    pieces = pl.pallas_call(
        pick_kernel,
        out_shape=jax.ShapeDtypeStruct((16, 8, tile_size), jnp.bfloat16),
        in_specs=[whole(pltpu.SMEM), whole()],
        out_specs=whole(),
        compiler_params=pltpu.CompilerParams(vmem_limit_bytes=8 << 20),
        cost_estimate=pl.CostEstimate(flops=10_000, bytes_accessed=100_000, transcendentals=0),
    )(depth_owner, pieces)
    pieces = exchange(pieces, ("y4", "y2", "h", "c"))
    half = jax.ShapeDtypeStruct((2, slots // 2, 8, tile_size), jnp.bfloat16)
    own, other, factors = pl.pallas_call(
        pack_kernel,
        out_shape=(half, half, jax.ShapeDtypeStruct((slots // 2, 8, tile_size), jnp.float32)),
        in_specs=[whole(pltpu.SMEM)] + [whole()] * 2,
        out_specs=(whole(), whole(), whole()),
        compiler_params=pltpu.CompilerParams(vmem_limit_bytes=8 << 20),
        cost_estimate=pl.CostEstimate(flops=300_000, bytes_accessed=1_300_000, transcendentals=0),
    )(freq_ids, wavefield, other)
    place = owner // 32 * 4 + lax.axis_index(("y4", "y2")).astype(jnp.int32)
    lensed = pl.pallas_call(
        lens_kernel,
        out_shape=jax.ShapeDtypeStruct((8 * slots, 2 * tile_size), jnp.bfloat16),
        in_specs=[whole(pltpu.SMEM)] + [whole()] * 4,
        out_specs=whole(pl.ANY),
        scratch_shapes=[pltpu.VMEM((8 * slots, 2 * tile_size), jnp.bfloat16), pltpu.SemaphoreType.DMA((4,))],
        compiler_params=pltpu.CompilerParams(vmem_limit_bytes=8 << 20),
        cost_estimate=pl.CostEstimate(flops=6_000_000, bytes_accessed=1_300_000, transcendentals=0),
    )(jnp.stack([place, side]), pieces, own, other, factors)
    columns = exchange(lensed.reshape(slots, 8, 2 * tile_size), freq)

    table_cos, table_sin = dft_table(size)
    shift = pl.pallas_call(
        shift_kernel,
        out_shape=jax.ShapeDtypeStruct((2, size, size), jnp.bfloat16),
        in_specs=[whole(pltpu.SMEM)] * 2,
        out_specs=whole(),
        compiler_params=pltpu.CompilerParams(vmem_limit_bytes=16 << 20),
        cost_estimate=pl.CostEstimate(flops=10_000_000, bytes_accessed=2_100_000, transcendentals=500_000),
    )(lax.axis_index(freq).astype(jnp.int32)[None], freq_ids)
    columns, shift = lax.optimization_barrier((columns, shift))

    table_cos, table_sin = jnp.asarray(table_cos), jnp.asarray(table_sin)
    own = pl.pallas_call(
        column_kernel,
        out_shape=jax.ShapeDtypeStruct((2, 2, size, tile_size), jnp.bfloat16),
        in_specs=[whole()] * 3,
        out_specs=whole(),
        scratch_shapes=[pltpu.VMEM((size, 4 * tile_size), jnp.bfloat16)],
        compiler_params=pltpu.CompilerParams(vmem_limit_bytes=8 << 20),
        cost_estimate=pl.CostEstimate(flops=540_000_000, bytes_accessed=2_100_000, transcendentals=0),
    )(table_cos, table_sin, columns)
    beside = lax.ppermute(own, "c", swap)
    near = pl.pallas_call(
        near_kernel,
        out_shape=jax.ShapeDtypeStruct((2, size, size), jnp.float32),
        in_specs=[whole(pltpu.SMEM)] + [whole()] * 3,
        out_specs=whole(),
        scratch_shapes=[pltpu.VMEM((2, size, 2 * tile_size), jnp.bfloat16)],
        compiler_params=pltpu.CompilerParams(vmem_limit_bytes=12 << 20),
        cost_estimate=pl.CostEstimate(flops=540_000_000, bytes_accessed=3_600_000, transcendentals=0),
    )(tile[None], own, table_cos, table_sin)
    wave_next, parts = pl.pallas_call(
        step_kernel,
        out_shape=(
            jax.ShapeDtypeStruct((2, tile_size, size), jnp.bfloat16),
            jax.ShapeDtypeStruct((size, tile_size), jnp.bfloat16),
        ),
        in_specs=[whole(pltpu.SMEM)] + [whole()] * 5,
        out_specs=(whole(pl.ANY), whole()),
        scratch_shapes=[
            pltpu.VMEM((2, size, 2 * tile_size), jnp.bfloat16),
            pltpu.VMEM((2 * tile_size, size), jnp.bfloat16),
            pltpu.VMEM((2, tile_size, size), jnp.bfloat16),
            pltpu.SemaphoreType.DMA,
        ],
        compiler_params=pltpu.CompilerParams(vmem_limit_bytes=20 << 20),
        cost_estimate=pl.CostEstimate(flops=1_080_000_000, bytes_accessed=5_600_000, transcendentals=0),
    )(tile[None], near, beside, table_cos, table_sin, shift)
    parts = exchange(parts.reshape(slots, size // slots, tile_size), freq)
    image = jnp.sum(parts.astype(jnp.float32), axis=0).T
    return (wave_next[:, None], image)


def solution(mesh):
    grid = Mesh(mesh.devices.reshape((2,) * 9), freq + ("h", "c"))
    tile = ("h", "c")
    return jax.shard_map(
        local,
        mesh=grid,
        in_specs=(P(None, None, freq, tile), P(freq, tile, None), P(), P()),
        out_specs=(P(None, freq, tile, None), P(tile, freq)),
        check_vma=False,
    )
```

```python
import math

import jax
import jax.numpy as jnp
import numpy as np
from jax import lax
from jax.experimental import pallas as pl
from jax.experimental.pallas import tpu as pltpu
from jax.sharding import Mesh
from jax.sharding import PartitionSpec as P

depth_step = 0.5
omega_top = 2.8
slots = 128
size = 512
tile_size = 128
freq = ("y4", "y2", "y1", "w", "z4", "z2", "z1")
mixed = ("z1", "y1", "w", "z2", "y2", "z4", "y4")


def place_of(slot):
    bits = {axis: slot >> (len(freq) - 1 - at) & 1 for at, axis in enumerate(freq)}
    return sum(bits[axis] << (len(mixed) - 1 - at) for at, axis in enumerate(mixed))


def dft_table(length):
    places = np.arange(length)
    angles = 2.0 * np.pi / length * (places[:, None] * places[None, :] % length)
    factor = 1.0 / math.sqrt(length)
    return (
        (np.cos(angles) * factor).astype(jnp.bfloat16),
        (np.sin(angles) * factor).astype(jnp.bfloat16),
    )


def dot(left, right):
    return jnp.dot(left, right, preferred_element_type=jnp.float32)


def series(square, first, last):
    total = (-1.0) ** ((last - first) // 2) / math.factorial(last)
    for order in range(last - 2, first - 1, -2):
        total = (-1.0) ** ((order - first) // 2) / math.factorial(order) + square * total
    return total


def rows_kernel(slow_ref, out_ref):
    for at in range(0, 32, 4):
        slow = slow_ref[0, 4 * at : 4 * at + 16, :].astype(jnp.float32)
        for k in range(4):
            out_ref[at + k] = slow[4 * k : 4 * k + 4].astype(jnp.bfloat16)


def pick_kernel(owner_ref, rows_ref, out_ref):
    rows = rows_ref[owner_ref[0] % 32].astype(jnp.float32)
    for c in range(2):
        lanes = (c * tile_size, (2 + c) * tile_size)
        piece = jnp.concatenate([rows[:, lane : lane + tile_size] for lane in lanes], axis=0).astype(jnp.bfloat16)
        for u in range(4):
            for h in range(2):
                out_ref[(u * 2 + h) * 2 + c] = piece


def shift_kernel(slot_ref, ids_ref, shift_ref):
    angular = omega_top * (ids_ref[slot_ref[0]] + 1).astype(jnp.float32) / slots

    def square(start, shape, axis):
        places = lax.broadcasted_iota(jnp.int32, shape, axis) + start
        signed = jnp.where(places < size // 2, places, places - size)
        return (2.0 * math.pi / size * signed.astype(jnp.float32)) ** 2

    ky_square = square(0, (16, size), 1)

    @pl.loop(0, size, step=16)
    def _(start):
        start = pl.multiple_of(start, 16)
        vertical = angular * angular - square(start, (16, size), 0) - ky_square
        root = depth_step * jnp.sqrt(jnp.abs(vertical))
        travel = jnp.where(vertical > 0.0, root, 0.0)
        damping = jnp.exp(jnp.where(vertical < 0.0, -root, 0.0))
        travel_square = travel * travel
        shift_ref[0, pl.ds(start, 16), :] = (damping * series(travel_square, 0, 12)).astype(jnp.bfloat16)
        shift_ref[1, pl.ds(start, 16), :] = (damping * travel * series(travel_square, 1, 13)).astype(jnp.bfloat16)


def pack_kernel(ids_ref, own_ref, other_ref, own_out, other_out, factor_ref):
    own_out[...] = own_ref[...]
    other_out[...] = other_ref[...]
    first = lax.broadcasted_iota(jnp.int32, (8, tile_size), 0) < 4
    for pair in range(slots // 2):
        low, high = (
            depth_step * (omega_top * (ids_ref[2 * pair + at] + 1).astype(jnp.float32) / slots) for at in range(2)
        )
        factor_ref[pair] = jnp.where(first, low, high)


def lens_kernel(place_ref, slow_ref, own_ref, other_ref, factor_ref, out_ref):
    slow = slow_ref[place_ref[0]].astype(jnp.float32) - 1.0
    halves = (jnp.concatenate([slow[:4]] * 2, axis=0), jnp.concatenate([slow[4:]] * 2, axis=0))
    low = place_ref[1] == 0
    depths = (jnp.where(low, halves[0], halves[1]), jnp.where(low, halves[1], halves[0]))
    for pair in range(slots // 2):
        factor = factor_ref[pair]
        for block, (ref, depth) in enumerate(zip((own_ref, other_ref), depths)):
            phase = factor * depth
            square = phase * phase
            lens_cos = series(square, 0, 8)
            lens_sin = phase * series(square, 1, 9)
            wave_real = ref[0, pair].astype(jnp.float32)
            wave_imag = ref[1, pair].astype(jnp.float32)
            real = wave_real * lens_cos - wave_imag * lens_sin
            imag = wave_real * lens_sin + wave_imag * lens_cos
            lanes = slice(block * tile_size, (block + 1) * tile_size)
            out_ref[place_of(2 * pair), :, lanes] = jnp.concatenate([real[:4], imag[:4]], axis=0).astype(jnp.bfloat16)
            out_ref[place_of(2 * pair + 1), :, lanes] = jnp.concatenate([real[4:], imag[4:]], axis=0).astype(jnp.bfloat16)


def column_kernel(cos_ref, sin_ref, wave_ref, out_ref, both):
    for at in range(0, size // 4, 4):
        tiles = [wave_ref[place_of(at + k)].astype(jnp.float32) for k in range(4)]
        for part in range(2):
            rows = jnp.concatenate([tile[4 * part : 4 * part + 4] for tile in tiles], axis=0)
            both[4 * at : 4 * at + 16, part * 2 * tile_size : (part + 1) * 2 * tile_size] = rows.astype(jnp.bfloat16)
    by_cos = dot(cos_ref[...], both[...])
    by_sin = dot(sin_ref[...], both[...])
    real = (by_cos[:, : 2 * tile_size] + by_sin[:, 2 * tile_size :]).astype(jnp.bfloat16)
    imag = (by_cos[:, 2 * tile_size :] - by_sin[:, : 2 * tile_size]).astype(jnp.bfloat16)
    for block in range(2):
        lanes = slice(block * tile_size, (block + 1) * tile_size)
        out_ref[block, 0] = real[:, lanes]
        out_ref[block, 1] = imag[:, lanes]


def half_transform(tile, flips, block_ref, cos_ref, sin_ref, field, use):
    starts = [pl.multiple_of((tile ^ flip) * tile_size, tile_size) for flip in flips]
    for at in range(2):
        field[:, :, at * tile_size : (at + 1) * tile_size] = block_ref[at]
    cos_rows, sin_rows = (
        jnp.concatenate([ref[pl.ds(start, tile_size), :] for start in starts], axis=0) for ref in (cos_ref, sin_ref)
    )
    width = 512
    for at in range(0, size, width):
        part = slice(at, at + width)
        real = dot(field[0], cos_rows[:, part]) + dot(field[1], sin_rows[:, part])
        imag = dot(field[1], cos_rows[:, part]) - dot(field[0], sin_rows[:, part])
        use(part, real, imag)


def near_kernel(tile_ref, own_ref, cos_ref, sin_ref, out_ref, field):
    def use(part, real, imag):
        out_ref[0, :, part] = real
        out_ref[1, :, part] = imag

    half_transform(tile_ref[0], (0, 2), own_ref, cos_ref, sin_ref, field, use)


def step_kernel(tile_ref, near_ref, other_ref, cos_ref, sin_ref, shift_ref, wave_ref, image_ref, field, back):
    tile = tile_ref[0]
    rows = pl.ds(pl.multiple_of(tile * tile_size, tile_size), tile_size)
    inverse = jnp.concatenate([cos_ref[rows, :], sin_ref[rows, :]], axis=0)
    width = 256

    def use(part, real, imag):
        spec_real = real + near_ref[0, :, part]
        spec_imag = imag + near_ref[1, :, part]
        shift_real = shift_ref[0, :, part].astype(jnp.float32)
        shift_imag = shift_ref[1, :, part].astype(jnp.float32)
        shifted_real = (spec_real * shift_real - spec_imag * shift_imag).astype(jnp.bfloat16)
        shifted_imag = (spec_real * shift_imag + spec_imag * shift_real).astype(jnp.bfloat16)
        from_real = dot(inverse, shifted_real)
        from_imag = dot(inverse, shifted_imag)
        back[:tile_size, part] = (from_real[:tile_size] - from_imag[tile_size:]).astype(jnp.bfloat16)
        back[tile_size:, part] = (from_imag[:tile_size] + from_real[tile_size:]).astype(jnp.bfloat16)

    half_transform(tile, (1, 3), other_ref, cos_ref, sin_ref, field, use)
    for at in range(0, size, width):
        part = slice(at, at + width)
        by_cos = dot(back[...], cos_ref[:, part])
        by_sin = dot(back[...], sin_ref[:, part])
        field_real = by_cos[:tile_size] - by_sin[tile_size:]
        wave_ref[0, :, part] = field_real.astype(jnp.bfloat16)
        wave_ref[1, :, part] = (by_cos[tile_size:] + by_sin[:tile_size]).astype(jnp.bfloat16)
        image = (field_real * (1.0 / math.sqrt(slots))).T.astype(jnp.bfloat16)
        for slot in range(at // 4, (at + width) // 4):
            image_ref[place_of(slot)] = image[4 * slot - at : 4 * slot - at + 4]


def whole(memory=pltpu.VMEM):
    return pl.BlockSpec(memory_space=memory)


def exchange(x, axes):
    return lax.all_to_all(x, axes, split_axis=0, concat_axis=0, tiled=True)


def local(wavefield, slowness, freq_ids, depth_owner):
    owner = depth_owner[0]
    swap = [(0, 1), (1, 0)]
    side = lax.axis_index("h").astype(jnp.int32)
    tile = 2 * side + lax.axis_index("c").astype(jnp.int32)
    wavefield = wavefield.reshape(2, slots // 2, 8, tile_size)
    pieces = pl.pallas_call(
        rows_kernel,
        out_shape=jax.ShapeDtypeStruct((32, 4, size), jnp.bfloat16),
        in_specs=[whole()],
        out_specs=whole(),
        compiler_params=pltpu.CompilerParams(vmem_limit_bytes=8 << 20),
        cost_estimate=pl.CostEstimate(flops=10_000, bytes_accessed=260_000, transcendentals=0),
    )(slowness)
    pieces = exchange(pieces, ("y1", "w", "z4", "z2", "z1"))
    other = lax.ppermute(wavefield, "h", swap)
    pieces = pl.pallas_call(
        pick_kernel,
        out_shape=jax.ShapeDtypeStruct((16, 8, tile_size), jnp.bfloat16),
        in_specs=[whole(pltpu.SMEM), whole()],
        out_specs=whole(),
        compiler_params=pltpu.CompilerParams(vmem_limit_bytes=8 << 20),
        cost_estimate=pl.CostEstimate(flops=10_000, bytes_accessed=100_000, transcendentals=0),
    )(depth_owner, pieces)
    pieces = exchange(pieces, ("y4", "y2", "h", "c"))
    half = jax.ShapeDtypeStruct((2, slots // 2, 8, tile_size), jnp.bfloat16)
    own, other, factors = pl.pallas_call(
        pack_kernel,
        out_shape=(half, half, jax.ShapeDtypeStruct((slots // 2, 8, tile_size), jnp.float32)),
        in_specs=[whole(pltpu.SMEM)] + [whole()] * 2,
        out_specs=(whole(), whole(), whole()),
        compiler_params=pltpu.CompilerParams(vmem_limit_bytes=8 << 20),
        cost_estimate=pl.CostEstimate(flops=300_000, bytes_accessed=1_300_000, transcendentals=0),
    )(freq_ids, wavefield, other)
    place = owner // 32 * 4 + lax.axis_index(("y4", "y2")).astype(jnp.int32)
    lensed = pl.pallas_call(
        lens_kernel,
        out_shape=jax.ShapeDtypeStruct((slots, 8, 2 * tile_size), jnp.bfloat16),
        in_specs=[whole(pltpu.SMEM)] + [whole()] * 4,
        out_specs=whole(),
        compiler_params=pltpu.CompilerParams(vmem_limit_bytes=8 << 20),
        cost_estimate=pl.CostEstimate(flops=6_000_000, bytes_accessed=1_300_000, transcendentals=0),
    )(jnp.stack([place, side]), pieces, own, other, factors)
    columns = exchange(lensed, mixed)

    table_cos, table_sin = dft_table(size)
    shift = pl.pallas_call(
        shift_kernel,
        out_shape=jax.ShapeDtypeStruct((2, size, size), jnp.bfloat16),
        in_specs=[whole(pltpu.SMEM)] * 2,
        out_specs=whole(),
        compiler_params=pltpu.CompilerParams(vmem_limit_bytes=16 << 20),
        cost_estimate=pl.CostEstimate(flops=10_000_000, bytes_accessed=2_100_000, transcendentals=500_000),
    )(lax.axis_index(freq).astype(jnp.int32)[None], freq_ids)
    columns, shift = lax.optimization_barrier((columns, shift))

    table_cos, table_sin = jnp.asarray(table_cos), jnp.asarray(table_sin)
    own = pl.pallas_call(
        column_kernel,
        out_shape=jax.ShapeDtypeStruct((2, 2, size, tile_size), jnp.bfloat16),
        in_specs=[whole()] * 3,
        out_specs=whole(),
        scratch_shapes=[pltpu.VMEM((size, 4 * tile_size), jnp.bfloat16)],
        compiler_params=pltpu.CompilerParams(vmem_limit_bytes=8 << 20),
        cost_estimate=pl.CostEstimate(flops=540_000_000, bytes_accessed=2_100_000, transcendentals=0),
    )(table_cos, table_sin, columns)
    beside = lax.ppermute(own, "c", swap)
    near = pl.pallas_call(
        near_kernel,
        out_shape=jax.ShapeDtypeStruct((2, size, size), jnp.float32),
        in_specs=[whole(pltpu.SMEM)] + [whole()] * 3,
        out_specs=whole(),
        scratch_shapes=[pltpu.VMEM((2, size, 2 * tile_size), jnp.bfloat16)],
        compiler_params=pltpu.CompilerParams(vmem_limit_bytes=12 << 20),
        cost_estimate=pl.CostEstimate(flops=540_000_000, bytes_accessed=3_600_000, transcendentals=0),
    )(tile[None], own, table_cos, table_sin)
    wave_next, parts = pl.pallas_call(
        step_kernel,
        out_shape=(
            jax.ShapeDtypeStruct((2, tile_size, size), jnp.bfloat16),
            jax.ShapeDtypeStruct((slots, size // slots, tile_size), jnp.bfloat16),
        ),
        in_specs=[whole(pltpu.SMEM)] + [whole()] * 5,
        out_specs=(whole(), whole()),
        scratch_shapes=[
            pltpu.VMEM((2, size, 2 * tile_size), jnp.bfloat16),
            pltpu.VMEM((2 * tile_size, size), jnp.bfloat16),
        ],
        compiler_params=pltpu.CompilerParams(vmem_limit_bytes=20 << 20),
        cost_estimate=pl.CostEstimate(flops=1_080_000_000, bytes_accessed=5_600_000, transcendentals=0),
    )(tile[None], near, beside, table_cos, table_sin, shift)
    parts = exchange(parts, mixed)
    image = jnp.sum(parts.astype(jnp.float32), axis=0).T
    return (wave_next[:, None], image)


def solution(mesh):
    grid = Mesh(mesh.devices.reshape((2,) * 9), freq + ("h", "c"))
    tile = ("h", "c")
    return jax.shard_map(
        local,
        mesh=grid,
        in_specs=(P(None, None, freq, tile), P(freq, tile, None), P(), P()),
        out_specs=(P(None, freq, tile, None), P(tile, freq)),
        check_vma=False,
    )
```
